32 devices in a mesh: energy: 4 (over z), slab: 8 (over y, x, core).
Axes of the slice: x: 2, y: 2, z: 4, core: 2. Of those that a mesh axis runs over, the one named last changes fastest.
Arguments:
- wavefunction: bfloat16 [4, 128, 64, 256], P('energy', 'slab'), may hold values from -6 to 6
- injected_modes: int32 [4, 64], P('energy'), may hold values from 0 to 255, all different within a row
- factor_blocks: float32 [4, 128, 256, 256], P('energy', 'slab'), may hold values from -1.1 to 1.1
- pivot_inverse: float32 [4, 128, 256, 256], P('energy', 'slab'), may hold values from -1 to 2.5
- mode_velocity: float32 [4, 256], P('energy'), may hold values from 0.1 to 1
- energy_weight: float32 [4], P('energy'), may hold values from 0.5 to 8
- mode_basis: bfloat16 [256, 1024], replicated, may hold values from -0.375 to 0.375
Outputs:
- sensitivity: float32 [1024, 128], P('energy', 'slab')
The draws below stay inside these ranges and needn't reach their ends.
Inputs may be any that keep to these rules, and one draw needn't show every extreme that they name: `injected_modes`: each energy's row names 64 different modes, and every mode is named by some energy.
All inputs are finite; a program needn't handle non-finite values.
Results may differ from the reference program's by a relative error of at most 0.0003.
Values sent between devices are 32-bit elements; how exact they have to be, the bound alone decides.
A program may use at most 128 MiB of HBM per device.

```python
import math
import jax
import jax.numpy as jnp
from jax import lax

M = 256
C = 64
G = 1024
SLAB_DEV = 16
ENERGY_GROUPS = 4
WIRE_SLABS = 128


def draw_factor_blocks(key, part):
    random_keys = jax.random.split(key, 7)
    slow_share = 0.5
    sluggish_part = jax.random.uniform(random_keys[0], (ENERGY_GROUPS, 1, M)) < slow_share
    fast_length = SLAB_DEV * jax.random.uniform(random_keys[1], (ENERGY_GROUPS, 1, M), minval=2.0, maxval=3.0)
    slow_length = WIRE_SLABS * jax.random.uniform(random_keys[2], (ENERGY_GROUPS, 1, M), minval=1.0, maxval=3.0)
    length = jnp.where(sluggish_part, slow_length, fast_length)
    spread = jnp.exp(jax.random.uniform(random_keys[3], (ENERGY_GROUPS, WIRE_SLABS, M), minval=-0.35, maxval=0.35))
    damping_rate = jnp.exp(-spread / length)
    sudden_spike = jax.random.uniform(random_keys[4], (ENERGY_GROUPS, WIRE_SLABS, 1)) < 3.0 / WIRE_SLABS
    loss_values = jax.random.uniform(random_keys[5], (ENERGY_GROUPS, WIRE_SLABS, M), minval=0.5, maxval=0.8)
    damping_rate = damping_rate * jnp.where(jnp.logical_and(sudden_spike, sluggish_part), loss_values, 1.0)
    mixing = jnp.clip(jax.random.normal(random_keys[6], (ENERGY_GROUPS, WIRE_SLABS, M, M)), -4.0, 4.0) * (0.1 / math.sqrt(M))
    return mixing + jnp.eye(M, dtype=jnp.float32) * damping_rate[..., None]


def draw_pivot_inverse(key, part):
    random_keys = jax.random.split(key, 2)
    diagonal = jax.random.uniform(random_keys[0], (ENERGY_GROUPS, WIRE_SLABS, M), minval=0.5, maxval=1.5)
    mixing = jnp.clip(jax.random.normal(random_keys[1], (ENERGY_GROUPS, WIRE_SLABS, M, M)), -4.0, 4.0) * (0.3 / math.sqrt(M))
    return mixing + jnp.eye(M, dtype=jnp.float32) * diagonal[..., None]


def draw_wavefunction(key, part):
    position = jnp.arange(WIRE_SLABS, dtype=jnp.float32) / WIRE_SLABS
    amplitude = (0.5 + position)[None, :, None, None]
    values = jnp.clip(jax.random.normal(key, (ENERGY_GROUPS, WIRE_SLABS, C, M)), -4.0, 4.0) * amplitude
    return values.astype(jnp.bfloat16)


def draw_energy_weight(key, part):
    level = jnp.arange(ENERGY_GROUPS, dtype=jnp.float32) / max(ENERGY_GROUPS - 1, 1)
    values = (1.0 + 2.0 * level) * jnp.exp(jax.random.uniform(key, (ENERGY_GROUPS,), minval=-0.2, maxval=0.2))
    return values


def shard_levels(key, dims, cuts, least, largest):
    def one(axis_at, shards_of):
        heights = jax.random.uniform(jax.random.fold_in(jax.random.fold_in(key, 6), axis_at), (shards_of,), jnp.float32, least / len(cuts), largest / len(cuts))
        return jnp.repeat(jnp.exp(heights), dims[axis_at] // shards_of).reshape((-1,) + (1,) * (len(dims) - axis_at - 1))

    factor_of = one(*cuts[0])
    for cut in cuts[1:]:
        factor_of = factor_of * one(*cut)
    return factor_of


def distinct(key, rows, amount, top, lift):
    ranking = jax.random.permutation(jax.random.fold_in(key, 1), amount)
    pull = ranking
    for power in range(3):
        pull = pull * pull // amount
    pull = pull * lift // amount
    chance = jax.random.randint(jax.random.fold_in(key, 2), (rows, amount), 0, 4096) + pull
    sure = jax.random.permutation(jax.random.fold_in(key, 3), rows)[jnp.arange(amount) % rows]
    chance = jnp.where(jnp.arange(rows)[:, None] == sure[None, :], 1 << 14, chance)
    merit = chance * amount + jnp.arange(amount)
    return lax.top_k(merit.astype(jnp.int32), top)[1].astype(jnp.int32)


def gaussian(own_key, dims, scale, bound, held_as=jnp.bfloat16):
    drawn = scale * jax.random.normal(own_key, dims, jnp.float32)
    return jnp.clip(drawn, min=-bound, max=bound).astype(held_as)


def setup_inputs(seed: int = 0) -> dict:
    streams_of = jax.random.split(jax.random.key(seed), 8)
    return {
        "wavefunction": draw_wavefunction(jax.random.fold_in(streams_of[7], 71), 0),
        "injected_modes": distinct(streams_of[1], ENERGY_GROUPS, M, C, 0),
        "factor_blocks": draw_factor_blocks(jax.random.fold_in(streams_of[7], 71), 0),
        "pivot_inverse": draw_pivot_inverse(jax.random.fold_in(streams_of[7], 71), 0),
        "mode_velocity": jnp.clip(jnp.exp(math.log(1.0) - 2.3025851 * jax.random.uniform(streams_of[4], (ENERGY_GROUPS, M), jnp.float32) ** shard_levels(streams_of[4], (ENERGY_GROUPS, M), ((0, 4),), -0.2, 0.2)), 0.1, 1.0),
        "energy_weight": draw_energy_weight(jax.random.fold_in(streams_of[7], 71), 0),
        "mode_basis": gaussian(streams_of[6], (M, G), M ** -0.5, 0.375),
    }


def reference(wavefunction, injected_modes, factor_blocks, pivot_inverse, mode_velocity, energy_weight, mode_basis):
    highest = lax.Precision.HIGHEST
    picked = jnp.take_along_axis(mode_velocity, injected_modes.astype(jnp.int32), axis=1)
    column_weight = 1.0 / picked
    wave_float = wavefunction.astype(jnp.float32)
    scaled = energy_weight[:, None, None] * column_weight[:, :, None] * mode_velocity[:, None, :]
    current = jnp.sum(scaled[:, None] * wave_float * wave_float) / WIRE_SLABS
    basis_float = mode_basis.astype(jnp.float32)
    empty = jnp.zeros((C, M), jnp.float32)

    def forward_step(carried, pieces):
        source_row, factor, pivot_block = pieces
        current_state = source_row + carried
        return (jnp.dot(current_state, factor, precision=highest, preferred_element_type=jnp.float32),
                jnp.dot(current_state, pivot_block, precision=highest, preferred_element_type=jnp.float32))

    def backward_step(carried, pieces):
        weighted_row, factor = pieces
        current_state = weighted_row + jnp.dot(carried, factor.T, precision=highest, preferred_element_type=jnp.float32)
        return current_state, current_state

    total_grad = jnp.zeros((WIRE_SLABS, G), jnp.float32)
    for energy in range(ENERGY_GROUPS):
        source = (2.0 / (WIRE_SLABS * current)) * scaled[energy][None] * wave_float[energy]
        weighted = lax.scan(forward_step, empty, (source, factor_blocks[energy], pivot_inverse[energy]))[1]
        adjoint = lax.scan(backward_step, empty, (weighted, factor_blocks[energy]), reverse=True)[1]
        wave_grid = jnp.dot(wavefunction[energy].reshape(WIRE_SLABS * C, M), mode_basis, preferred_element_type=jnp.float32)
        adjoint_grid = jnp.dot(adjoint.reshape(WIRE_SLABS * C, M), basis_float, precision=highest, preferred_element_type=jnp.float32)
        total_grad = total_grad + jnp.sum((wave_grid * adjoint_grid).reshape(WIRE_SLABS, C, G), axis=1)
    return (WIRE_SLABS * G) * total_grad.T
```

```python
import functools
import jax
import jax.numpy as jnp
from jax import lax
from jax.experimental import pallas as pl
from jax.experimental.pallas import tpu as pltpu
from jax.sharding import PartitionSpec as P

F32 = jnp.float32
BF16 = jnp.bfloat16
MESH = pl.DeviceIdType.MESH


def split(x):
    hi = x.astype(BF16)
    return hi, (x - hi.astype(F32)).astype(BF16)


def dot(a, b, transposed=False):
    return lax.dot_general(
        a, b, (((1,), (1 if transposed else 0,)), ((), ())), preferred_element_type=F32
    )


def mm(a, bh, bl, transposed=False):
    ah, al = split(a)
    rows = a.shape[0]
    both = dot(jnp.concatenate([ah, al], axis=0), bh, transposed)
    return both[:rows] + both[rows:] + dot(ah, bl, transposed)


def kernel(
    n, groups,
    wave, inj, fac, piv, vel, ew, basis,
    out,
    fh, fl, qh, ql, uh, ul, th, tl, state, wt, adj, wg, off, scaled_ref,
    inc, cur, ctot, fsend, frecv, bsend, brecv, esend, erecv,
    fs, fr, bs, br, es, er,
):
    me = lax.axis_index("slab")
    mine = lax.axis_index("energy")
    slabs, cols, modes = wave.shape
    grid = basis.shape[1]
    part = grid // groups
    all_slabs = n * slabs
    small = 2.0 / (all_slabs * cols * modes * groups * 4096.0)

    barrier = pltpu.get_barrier_semaphore()

    for k in (1, n - 1):
        pl.semaphore_signal(
            barrier, inc=1, device_id=(mine, lax.rem(me + k, n)), device_id_type=MESH
        )
    for k in range(1, groups):
        peer = lax.rem(mine + k, groups)
        pl.semaphore_signal(barrier, inc=1, device_id=(peer, me), device_id_type=MESH)

    rows_at = lax.broadcasted_iota(jnp.int32, (cols, cols), 0)
    cols_at = lax.broadcasted_iota(jnp.int32, (cols, cols), 1)
    picked = jnp.sum(
        jnp.where(rows_at == cols_at, jnp.broadcast_to(inj[...].astype(F32), (cols, cols)), 0.0),
        axis=1, keepdims=True,
    )
    mode_at = lax.broadcasted_iota(jnp.int32, (cols, modes), 1).astype(F32)
    velocity = jnp.broadcast_to(vel[...], (cols, modes))
    at_injected = jnp.sum(jnp.where(mode_at == picked, velocity, 0.0), axis=1, keepdims=True)
    scaled_ref[...] = ew[...] * (1.0 / at_injected) * velocity

    eye = (
        lax.broadcasted_iota(jnp.int32, (modes, modes), 0)
        == lax.broadcasted_iota(jnp.int32, (modes, modes), 1)
    ).astype(F32)

    off[0:modes] = eye
    off[modes:] = jnp.zeros((cols, modes), F32)
    cur[...] = jnp.zeros_like(cur)

    def chain(s, carry):
        w = wave[s].astype(F32)
        sw = scaled_ref[...] * w
        sq = sw * w
        part_sum = sq[0:8]
        for i in range(1, cols // 8):
            part_sum = part_sum + sq[8 * i : 8 * i + 8]
        tile = part_sum[:, 0:128]
        for i in range(1, modes // 128):
            tile = tile + part_sum[:, 128 * i : 128 * i + 128]
        cur[...] += tile
        own = off[modes:] + sw * small
        state[s] = own
        block = jnp.concatenate([off[0:modes], own], axis=0)
        bh, bl = split(block)
        qh[s] = bh[0:modes]
        ql[s] = bl[0:modes]
        h, l = split(fac[s])
        fh[s] = h
        fl[s] = l
        total = modes + cols
        both = dot(jnp.concatenate([bh, bl], axis=0), h)
        off[...] = both[:total] + both[total:] + dot(bh, l)
        return carry

    lax.fori_loop(0, slabs, chain, 0)
    h, l = split(off[0:modes])
    th[...] = h
    tl[...] = l

    pl.semaphore_wait(barrier, groups + 1)

    to_right = pltpu.make_async_remote_copy(
        src_ref=fsend, dst_ref=frecv, send_sem=fs, recv_sem=fr,
        device_id=(mine, lax.rem(me + 1, n)), device_id_type=MESH,
    )
    to_left = pltpu.make_async_remote_copy(
        src_ref=bsend, dst_ref=brecv, send_sem=bs, recv_sem=br,
        device_id=(mine, lax.rem(me + n - 1, n)), device_id_type=MESH,
    )

    @pl.when(me == 0)
    def _():
        inc[...] = jnp.zeros_like(inc)

    @pl.when(me > 0)
    def _():
        to_right.wait_recv()
        inc[...] = frecv[0:cols]
        cur[...] += frecv[cols : cols + 8, 0:128]

    @pl.when(me < n - 1)
    def _():
        fsend[0:cols] = mm(inc[...], th[...], tl[...]) + off[modes:]
        fsend[cols : cols + 8, 0:128] = cur[...]
        fsend[cols : cols + 8, 128:] = jnp.zeros((8, modes - 128), F32)
        to_right.start()

    def weigh(s, carry):
        now = state[s] + mm(inc[...], qh[s], ql[s])
        h, l = split(piv[s])
        wt[s] = mm(now, h, l)
        return carry

    lax.fori_loop(0, slabs, weigh, 0)

    def back(i, x):
        s = slabs - 1 - i
        x = wt[s] + mm(x, fh[s], fl[s], True)
        adj[s] = x
        return x

    exit_state = lax.fori_loop(0, slabs, back, jnp.zeros((cols, modes), F32))
    bsend[0:cols] = exit_state

    @pl.when(me == n - 1)
    def _():
        ctot[...] = cur[...]
        bsend[cols : cols + 8, 0:128] = ctot[...]
        bsend[cols : cols + 8, 128:] = jnp.zeros((8, modes - 128), F32)
        to_left.start()

    @pl.when(me < n - 1)
    def _():
        off[0:modes] = eye

        def suffix(i, carry):
            s = slabs - 1 - i
            u = mm(off[0:modes], fh[s], fl[s], True)
            off[0:modes] = u
            h, l = split(u)
            uh[s] = h
            ul[s] = l
            return carry

        lax.fori_loop(0, slabs, suffix, 0)

    def waves(s, carry):
        wg[s] = dot(wave[s], basis[...])
        return carry

    lax.fori_loop(0, slabs, waves, 0)

    @pl.when(me < n - 1)
    def _():
        to_left.wait_recv()
        inc[...] = brecv[0:cols]
        ctot[...] = brecv[cols : cols + 8, 0:128]

    @pl.when(jnp.logical_and(me > 0, me < n - 1))
    def _():
        bsend[0:cols] += mm(inc[...], th[...], tl[...], True)
        bsend[cols : cols + 8, 0:128] = ctot[...]
        bsend[cols : cols + 8, 128:] = jnp.zeros((8, modes - 128), F32)
        to_left.start()

    @pl.when(me < n - 1)
    def _():
        def join(s, carry):
            adj[s] += mm(inc[...], uh[s], ul[s])
            return carry

        lax.fori_loop(0, slabs, join, 0)

    def gradient(s, carry):
        ah, al = split(adj[s])
        ag = dot(jnp.concatenate([ah, al], axis=0), basis[...])
        row = jnp.sum(wg[s] * (ag[:cols] + ag[cols:]), axis=0, keepdims=True)
        for e in range(groups):
            esend[e, pl.ds(s, 1), :] = row[:, e * part : (e + 1) * part]
        return carry

    lax.fori_loop(0, slabs, gradient, 0)
    for e in range(groups):
        esend[e, slabs : slabs + 8, 0:128] = ctot[...]
        if part > 128:
            esend[e, slabs : slabs + 8, 128:] = jnp.zeros((8, part - 128), F32)

    copies = []
    for k in range(1, groups):
        peer = lax.rem(mine + k, groups)
        copies.append(
            pltpu.make_async_remote_copy(
                src_ref=esend.at[peer], dst_ref=erecv.at[k], send_sem=es.at[k], recv_sem=er.at[k],
                device_id=(peer, me), device_id_type=MESH,
            )
        )
        copies[-1].start()
    total = esend[mine]
    for k in range(1, groups):
        copies[k - 1].wait_recv()
        total = total + erecv[k]
    current = jnp.sum(total[slabs : slabs + 8, 0:128])
    factor = (all_slabs * grid * (2.0 / small)) / current
    out[...] = total[0:slabs] * factor
    for copy in copies:
        copy.wait_send()

    @pl.when(me < n - 1)
    def _():
        to_right.wait_send()

    @pl.when(me > 0)
    def _():
        to_left.wait_send()


def local(wavefunction, injected_modes, factor_blocks, pivot_inverse, mode_velocity, energy_weight, mode_basis):
    n = lax.axis_size("slab")
    groups = lax.axis_size("energy")
    _, slabs, cols, modes = wavefunction.shape
    grid = mode_basis.shape[1]
    part = grid // groups
    vmem = pl.BlockSpec(memory_space=pltpu.VMEM)
    result = pl.pallas_call(
        functools.partial(kernel, n, groups),
        out_shape=jax.ShapeDtypeStruct((slabs, part), F32),
        in_specs=[vmem] * 7,
        out_specs=vmem,
        scratch_shapes=[
            pltpu.VMEM((slabs, modes, modes), BF16),
            pltpu.VMEM((slabs, modes, modes), BF16),
            pltpu.VMEM((slabs, modes, modes), BF16),
            pltpu.VMEM((slabs, modes, modes), BF16),
            pltpu.VMEM((slabs, modes, modes), BF16),
            pltpu.VMEM((slabs, modes, modes), BF16),
            pltpu.VMEM((modes, modes), BF16),
            pltpu.VMEM((modes, modes), BF16),
            pltpu.VMEM((slabs, cols, modes), F32),
            pltpu.VMEM((slabs, cols, modes), F32),
            pltpu.VMEM((slabs, cols, modes), F32),
            pltpu.VMEM((slabs, cols, grid), F32),
            pltpu.VMEM((modes + cols, modes), F32),
            pltpu.VMEM((cols, modes), F32),
            pltpu.VMEM((cols, modes), F32),
            pltpu.VMEM((8, 128), F32),
            pltpu.VMEM((8, 128), F32),
            pltpu.VMEM((cols + 8, modes), F32),
            pltpu.VMEM((cols + 8, modes), F32),
            pltpu.VMEM((cols + 8, modes), F32),
            pltpu.VMEM((cols + 8, modes), F32),
            pltpu.VMEM((groups, slabs + 8, part), F32),
            pltpu.VMEM((groups, slabs + 8, part), F32),
            pltpu.SemaphoreType.DMA,
            pltpu.SemaphoreType.DMA,
            pltpu.SemaphoreType.DMA,
            pltpu.SemaphoreType.DMA,
            pltpu.SemaphoreType.DMA((groups,)),
            pltpu.SemaphoreType.DMA((groups,)),
        ],
        compiler_params=pltpu.CompilerParams(
            collective_id=0, has_side_effects=True, vmem_limit_bytes=56 * 1024 * 1024
        ),
    )(
        wavefunction[0],
        injected_modes,
        factor_blocks[0],
        pivot_inverse[0],
        mode_velocity,
        energy_weight.reshape(1, 1),
        mode_basis,
    )
    return result.T


def solution(mesh):
    return jax.shard_map(
        local,
        mesh=mesh,
        in_specs=(
            P("energy", "slab", None, None),
            P("energy", None),
            P("energy", "slab", None, None),
            P("energy", "slab", None, None),
            P("energy", None),
            P("energy"),
            P(),
        ),
        out_specs=P("energy", "slab"),
        check_vma=False,
    )
```

```python
import functools
import jax
import jax.numpy as jnp
from jax import lax
from jax.experimental import pallas as pl
from jax.experimental.pallas import tpu as pltpu
from jax.sharding import PartitionSpec as P

F32 = jnp.float32
BF16 = jnp.bfloat16
MESH = pl.DeviceIdType.MESH


def split(x):
    hi = x.astype(BF16)
    return hi, (x - hi.astype(F32)).astype(BF16)


def dot(a, b, transposed=False):
    return lax.dot_general(
        a, b, (((1,), (1 if transposed else 0,)), ((), ())), preferred_element_type=F32
    )


def mm(a, bh, bl, transposed=False):
    ah, al = split(a)
    rows = a.shape[0]
    both = dot(jnp.concatenate([ah, al], axis=0), bh, transposed)
    return both[:rows] + both[rows:] + dot(ah, bl, transposed)


def kernel(
    n, groups,
    wave, inj, fac, piv, vel, ew, basis,
    out,
    fh, fl, qh, ql, uh, ul, th, tl, state, wt, adj, wg, off, scaled_ref,
    inc, cur, ctot, ps, pr, osend, orecv, tsend, trecv, isend, irecv, xsend, xrecv,
    ysend, yrecv, jsend, jrecv, esend, erecv,
    pair_s, pair_r, os, our, ts, tr, is_, ir, xs, xr, ys, yr, js, jr, es, er,
):
    me = lax.axis_index("slab")
    mine = lax.axis_index("energy")
    slabs, cols, modes = wave.shape
    grid = basis.shape[1]
    part = grid // groups
    chips = n // 2
    chip = me // 2
    core = lax.rem(me, 2)
    other = me + 1 - 2 * core
    total = modes + cols
    all_slabs = n * slabs
    small = 2.0 / (all_slabs * cols * modes * groups * 4096.0)

    barrier = pltpu.get_barrier_semaphore()

    for k in range(1, n):
        pl.semaphore_signal(
            barrier, inc=1, device_id=(mine, lax.rem(me + k, n)), device_id_type=MESH
        )
    for k in range(1, groups):
        peer = lax.rem(mine + k, groups)
        pl.semaphore_signal(barrier, inc=1, device_id=(peer, me), device_id_type=MESH)

    rows_at = lax.broadcasted_iota(jnp.int32, (cols, cols), 0)
    cols_at = lax.broadcasted_iota(jnp.int32, (cols, cols), 1)
    picked = jnp.sum(
        jnp.where(rows_at == cols_at, jnp.broadcast_to(inj[...].astype(F32), (cols, cols)), 0.0),
        axis=1, keepdims=True,
    )
    mode_at = lax.broadcasted_iota(jnp.int32, (cols, modes), 1).astype(F32)
    velocity = jnp.broadcast_to(vel[...], (cols, modes))
    at_injected = jnp.sum(jnp.where(mode_at == picked, velocity, 0.0), axis=1, keepdims=True)
    scaled_ref[...] = ew[...] * (1.0 / at_injected) * velocity

    eye = (
        lax.broadcasted_iota(jnp.int32, (modes, modes), 0)
        == lax.broadcasted_iota(jnp.int32, (modes, modes), 1)
    ).astype(F32)

    off[0:modes] = eye
    off[modes:] = jnp.zeros((cols, modes), F32)
    cur[...] = jnp.zeros_like(cur)

    def chain(s, carry):
        w = wave[s].astype(F32)
        sw = scaled_ref[...] * w
        sq = sw * w
        part_sum = sq[0:8]
        for i in range(1, cols // 8):
            part_sum = part_sum + sq[8 * i : 8 * i + 8]
        tile = part_sum[:, 0:128]
        for i in range(1, modes // 128):
            tile = tile + part_sum[:, 128 * i : 128 * i + 128]
        cur[...] += tile
        own = off[modes:] + sw * small
        state[s] = own
        block = jnp.concatenate([off[0:modes], own], axis=0)
        bh, bl = split(block)
        qh[s] = bh[0:modes]
        ql[s] = bl[0:modes]
        h, l = split(fac[s])
        fh[s] = h
        fl[s] = l
        both = dot(jnp.concatenate([bh, bl], axis=0), h)
        off[...] = both[:total] + both[total:] + dot(bh, l)
        return carry

    lax.fori_loop(0, slabs, chain, 0)
    h, l = split(off[0:modes])
    th[...] = h
    tl[...] = l

    pl.semaphore_wait(barrier, n + groups - 2)

    def copy_to(source, target, send, receive, device):
        return pltpu.make_async_remote_copy(
            src_ref=source, dst_ref=target, send_sem=send, recv_sem=receive,
            device_id=(mine, device), device_id_type=MESH,
        )

    pair = copy_to(ps, pr, pair_s, pair_r, other)
    entry = copy_to(isend, irecv, is_, ir, other)
    leaving = copy_to(xsend, xrecv, xs, xr, other)
    joining = copy_to(jsend, jrecv, js, jr, other)

    def offset_to(j):
        return copy_to(osend, orecv.at[chip], os.at[j], our.at[chip], 2 * j + 1)

    def transfer_to(j, k):
        return copy_to(tsend, trecv.at[chip], ts.at[j], tr.at[chip], 2 * j + k)

    def exit_to(j):
        return copy_to(ysend, yrecv.at[chip], ys.at[j], yr.at[chip], 2 * j)

    def wait_transfer(j):
        copy_to(tsend, trecv.at[j], ts.at[j], tr.at[j], other).wait_recv()

    def wait_offset(j):
        copy_to(osend, orecv.at[j], os.at[j], our.at[j], other).wait_recv()

    def wait_exit(j):
        copy_to(ysend, yrecv.at[j], ys.at[j], yr.at[j], other).wait_recv()

    def put(ref, value, tile):
        ref[0:cols] = value
        ref[cols : cols + 8, 0:128] = tile
        ref[cols : cols + 8, 128:] = jnp.zeros((8, modes - 128), F32)

    inner = jnp.logical_and(chip > 0, chip < chips - 1)

    ps[0:total] = off[...]
    ps[total:, 0:128] = cur[...]
    ps[total:, 128:] = jnp.zeros((8, modes - 128), F32)
    pair.start()
    pair.wait_recv()
    cur[...] += pr[total:, 0:128]
    ctot[...] = cur[...]

    @pl.when(core == 1)
    def _():
        whole = mm(pr[0:total], th[...], tl[...])
        tsend[...] = whole[0:modes]
        put(osend, whole[modes:] + off[modes:], cur[...])
        for j in range(chips):
            @pl.when(j > chip)
            def _():
                offset_to(j).start()

        @pl.when(inner)
        def _():
            for j in range(chips):
                @pl.when(j > chip)
                def _():
                    transfer_to(j, 1).start()

                @pl.when(j < chip)
                def _():
                    transfer_to(j, 0).start()

    off[0:modes] = eye

    def suffix(i, carry):
        s = slabs - 1 - i
        u = mm(off[0:modes], fh[s], fl[s], True)
        off[0:modes] = u
        h, l = split(u)
        uh[s] = h
        ul[s] = l
        return carry

    lax.fori_loop(0, slabs, suffix, 0)

    inc[...] = jnp.zeros_like(inc)

    @pl.when(core == 1)
    def _():
        for j in range(chips - 1):
            @pl.when(chip > j)
            def _():
                if j > 0:
                    wait_transfer(j)
                wait_offset(j)
                if j == 0:
                    inc[...] = orecv[j, 0:cols]
                else:
                    h, l = split(trecv[j])
                    inc[...] = mm(inc[...], h, l) + orecv[j, 0:cols]
                ctot[...] += orecv[j, cols : cols + 8, 0:128]

        put(isend, inc[...], ctot[...])
        entry.start()
        h, l = split(pr[0:modes])
        inc[...] = mm(inc[...], h, l) + pr[modes:total]

    @pl.when(core == 0)
    def _():
        entry.wait_recv()
        inc[...] = irecv[0:cols]
        ctot[...] = irecv[cols : cols + 8, 0:128]

    def weigh(s, carry):
        now = state[s] + mm(inc[...], qh[s], ql[s])
        h, l = split(piv[s])
        wt[s] = mm(now, h, l)
        return carry

    lax.fori_loop(0, slabs, weigh, 0)

    def back(i, x):
        s = slabs - 1 - i
        x = wt[s] + mm(x, fh[s], fl[s], True)
        adj[s] = x
        return x

    exit_state = lax.fori_loop(0, slabs, back, jnp.zeros((cols, modes), F32))

    @pl.when(core == 1)
    def _():
        xsend[...] = exit_state
        leaving.start()

    @pl.when(core == 0)
    def _():
        leaving.wait_recv()

        @pl.when(chip > 0)
        def _():
            put(ysend, exit_state + mm(xrecv[...], th[...], tl[...], True), cur[...])
            for j in range(chips):
                @pl.when(j < chip)
                def _():
                    exit_to(j).start()

    def waves(s, carry):
        wg[s] = dot(wave[s], basis[...])
        return carry

    lax.fori_loop(0, slabs, waves, 0)

    @pl.when(core == 0)
    def _():
        inc[...] = jnp.zeros_like(inc)
        for j in range(chips - 1, 0, -1):
            @pl.when(chip < j)
            def _():
                if j < chips - 1:
                    wait_transfer(j)
                wait_exit(j)
                if j == chips - 1:
                    inc[...] = yrecv[j, 0:cols]
                else:
                    h, l = split(trecv[j])
                    inc[...] = mm(inc[...], h, l, True) + yrecv[j, 0:cols]
                ctot[...] += yrecv[j, cols : cols + 8, 0:128]

        put(jsend, inc[...], ctot[...])
        joining.start()
        h, l = split(pr[0:modes])
        inc[...] = mm(inc[...], h, l, True) + xrecv[...]

    @pl.when(core == 1)
    def _():
        joining.wait_recv()
        inc[...] = jrecv[0:cols]
        ctot[...] = jrecv[cols : cols + 8, 0:128]

    def join(s, carry):
        adj[s] += mm(inc[...], uh[s], ul[s])
        return carry

    lax.fori_loop(0, slabs, join, 0)

    def gradient(s, carry):
        ah, al = split(adj[s])
        ag = dot(jnp.concatenate([ah, al], axis=0), basis[...])
        row = jnp.sum(wg[s] * (ag[:cols] + ag[cols:]), axis=0, keepdims=True)
        for e in range(groups):
            esend[e, pl.ds(s, 1), :] = row[:, e * part : (e + 1) * part]
        return carry

    lax.fori_loop(0, slabs, gradient, 0)
    for e in range(groups):
        esend[e, slabs : slabs + 8, 0:128] = ctot[...]
        if part > 128:
            esend[e, slabs : slabs + 8, 128:] = jnp.zeros((8, part - 128), F32)

    copies = []
    for k in range(1, groups):
        peer = lax.rem(mine + k, groups)
        copies.append(
            pltpu.make_async_remote_copy(
                src_ref=esend.at[peer], dst_ref=erecv.at[k], send_sem=es.at[k], recv_sem=er.at[k],
                device_id=(peer, me), device_id_type=MESH,
            )
        )
        copies[-1].start()
    summed = esend[mine]
    for k in range(1, groups):
        copies[k - 1].wait_recv()
        summed = summed + erecv[k]
    current = jnp.sum(summed[slabs : slabs + 8, 0:128])
    factor = (all_slabs * grid * (2.0 / small)) / current
    out[...] = summed[0:slabs] * factor
    for copy in copies:
        copy.wait_send()

    pair.wait_send()

    @pl.when(core == 1)
    def _():
        entry.wait_send()
        leaving.wait_send()
        for j in range(chips):
            @pl.when(j > chip)
            def _():
                offset_to(j).wait_send()

        @pl.when(inner)
        def _():
            for j in range(chips):
                @pl.when(j > chip)
                def _():
                    transfer_to(j, 1).wait_send()

                @pl.when(j < chip)
                def _():
                    transfer_to(j, 0).wait_send()

    @pl.when(core == 0)
    def _():
        joining.wait_send()
        for j in range(chips):
            @pl.when(j < chip)
            def _():
                exit_to(j).wait_send()


def local(wavefunction, injected_modes, factor_blocks, pivot_inverse, mode_velocity, energy_weight, mode_basis):
    n = lax.axis_size("slab")
    groups = lax.axis_size("energy")
    _, slabs, cols, modes = wavefunction.shape
    grid = mode_basis.shape[1]
    part = grid // groups
    vmem = pl.BlockSpec(memory_space=pltpu.VMEM)
    result = pl.pallas_call(
        functools.partial(kernel, n, groups),
        out_shape=jax.ShapeDtypeStruct((slabs, part), F32),
        in_specs=[vmem] * 7,
        out_specs=vmem,
        scratch_shapes=[
            pltpu.VMEM((slabs, modes, modes), BF16),
            pltpu.VMEM((slabs, modes, modes), BF16),
            pltpu.VMEM((slabs, modes, modes), BF16),
            pltpu.VMEM((slabs, modes, modes), BF16),
            pltpu.VMEM((slabs, modes, modes), BF16),
            pltpu.VMEM((slabs, modes, modes), BF16),
            pltpu.VMEM((modes, modes), BF16),
            pltpu.VMEM((modes, modes), BF16),
            pltpu.VMEM((slabs, cols, modes), F32),
            pltpu.VMEM((slabs, cols, modes), F32),
            pltpu.VMEM((slabs, cols, modes), F32),
            pltpu.VMEM((slabs, cols, grid), F32),
            pltpu.VMEM((modes + cols, modes), F32),
            pltpu.VMEM((cols, modes), F32),
            pltpu.VMEM((cols, modes), F32),
            pltpu.VMEM((8, 128), F32),
            pltpu.VMEM((8, 128), F32),
            pltpu.VMEM((modes + cols + 8, modes), F32),
            pltpu.VMEM((modes + cols + 8, modes), F32),
            pltpu.VMEM((cols + 8, modes), F32),
            pltpu.VMEM((n // 2, cols + 8, modes), F32),
            pltpu.VMEM((modes, modes), F32),
            pltpu.VMEM((n // 2, modes, modes), F32),
            pltpu.VMEM((cols + 8, modes), F32),
            pltpu.VMEM((cols + 8, modes), F32),
            pltpu.VMEM((cols, modes), F32),
            pltpu.VMEM((cols, modes), F32),
            pltpu.VMEM((cols + 8, modes), F32),
            pltpu.VMEM((n // 2, cols + 8, modes), F32),
            pltpu.VMEM((cols + 8, modes), F32),
            pltpu.VMEM((cols + 8, modes), F32),
            pltpu.VMEM((groups, slabs + 8, part), F32),
            pltpu.VMEM((groups, slabs + 8, part), F32),
            pltpu.SemaphoreType.DMA,
            pltpu.SemaphoreType.DMA,
            pltpu.SemaphoreType.DMA((n // 2,)),
            pltpu.SemaphoreType.DMA((n // 2,)),
            pltpu.SemaphoreType.DMA((n // 2,)),
            pltpu.SemaphoreType.DMA((n // 2,)),
            pltpu.SemaphoreType.DMA,
            pltpu.SemaphoreType.DMA,
            pltpu.SemaphoreType.DMA,
            pltpu.SemaphoreType.DMA,
            pltpu.SemaphoreType.DMA((n // 2,)),
            pltpu.SemaphoreType.DMA((n // 2,)),
            pltpu.SemaphoreType.DMA,
            pltpu.SemaphoreType.DMA,
            pltpu.SemaphoreType.DMA((groups,)),
            pltpu.SemaphoreType.DMA((groups,)),
        ],
        compiler_params=pltpu.CompilerParams(
            collective_id=0, has_side_effects=True, vmem_limit_bytes=56 * 1024 * 1024
        ),
    )(
        wavefunction[0],
        injected_modes,
        factor_blocks[0],
        pivot_inverse[0],
        mode_velocity,
        energy_weight.reshape(1, 1),
        mode_basis,
    )
    return result.T


def solution(mesh):
    return jax.shard_map(
        local,
        mesh=mesh,
        in_specs=(
            P("energy", "slab", None, None),
            P("energy", None),
            P("energy", "slab", None, None),
            P("energy", "slab", None, None),
            P("energy", None),
            P("energy"),
            P(),
        ),
        out_specs=P("energy", "slab"),
        check_vma=False,
    )
```

```python
import functools
import jax
import jax.numpy as jnp
from jax import lax
from jax.experimental import pallas as pl
from jax.experimental.pallas import tpu as pltpu
from jax.sharding import PartitionSpec as P

F32 = jnp.float32
BF16 = jnp.bfloat16
MESH = pl.DeviceIdType.MESH


def split(x):
    hi = x.astype(BF16)
    return hi, (x - hi.astype(F32)).astype(BF16)


def dot(a, b, transposed=False):
    return lax.dot_general(
        a, b, (((1,), (1 if transposed else 0,)), ((), ())), preferred_element_type=F32
    )


def mm(a, bh, bl, transposed=False):
    ah, al = split(a)
    rows = a.shape[0]
    both = dot(jnp.concatenate([ah, al], axis=0), bh, transposed)
    return both[:rows] + both[rows:] + dot(ah, bl, transposed)


def kernel(
    n, groups,
    wave, inj, fac_hbm, piv_hbm, vel, ew, basis,
    out,
    fac, piv, ahl, fac_sem, piv_sem,
    fh, fl, qh, ql, uh, ul, th, tl, state, wt, adj, wg, off, scaled_ref,
    inc, cur, ctot, ps, pr, osend, orecv, tsend, trecv, isend, irecv, xsend, xrecv,
    ysend, yrecv, jsend, jrecv, esend, erecv,
    pair_s, pair_r, os, our, ts, tr, is_, ir, xs, xr, ys, yr, js, jr, es, er,
):
    me = lax.axis_index("slab")
    mine = lax.axis_index("energy")
    slabs, cols, modes = wave.shape
    grid = basis.shape[1]
    part = grid // groups
    chips = n // 2
    chip = me // 2
    core = lax.rem(me, 2)
    other = me + 1 - 2 * core
    total = modes + cols
    all_slabs = n * slabs
    small = 2.0 / (all_slabs * cols * modes * groups * 4096.0)

    def factor_in(s):
        return pltpu.make_async_copy(fac_hbm.at[s], fac.at[s], fac_sem.at[s])

    for s in range(slabs):
        factor_in(s).start()
    pivots_in = pltpu.make_async_copy(piv_hbm, piv, piv_sem)
    pivots_in.start()

    barrier = pltpu.get_barrier_semaphore()

    for k in range(1, n):
        pl.semaphore_signal(
            barrier, inc=1, device_id=(mine, lax.rem(me + k, n)), device_id_type=MESH
        )
    for k in range(1, groups):
        peer = lax.rem(mine + k, groups)
        pl.semaphore_signal(barrier, inc=1, device_id=(peer, me), device_id_type=MESH)

    rows_at = lax.broadcasted_iota(jnp.int32, (cols, cols), 0)
    cols_at = lax.broadcasted_iota(jnp.int32, (cols, cols), 1)
    picked = jnp.sum(
        jnp.where(rows_at == cols_at, jnp.broadcast_to(inj[...].astype(F32), (cols, cols)), 0.0),
        axis=1, keepdims=True,
    )
    mode_at = lax.broadcasted_iota(jnp.int32, (cols, modes), 1).astype(F32)
    velocity = jnp.broadcast_to(vel[...], (cols, modes))
    at_injected = jnp.sum(jnp.where(mode_at == picked, velocity, 0.0), axis=1, keepdims=True)
    scaled_ref[...] = ew[...] * (1.0 / at_injected) * velocity

    eye = (
        lax.broadcasted_iota(jnp.int32, (modes, modes), 0)
        == lax.broadcasted_iota(jnp.int32, (modes, modes), 1)
    ).astype(F32)

    off[0:modes] = eye
    off[modes:] = jnp.zeros((cols, modes), F32)
    cur[...] = jnp.zeros_like(cur)

    def chain(s, carry):
        w = wave[s].astype(F32)
        sw = scaled_ref[...] * w
        sq = sw * w
        part_sum = sq[0:8]
        for i in range(1, cols // 8):
            part_sum = part_sum + sq[8 * i : 8 * i + 8]
        tile = part_sum[:, 0:128]
        for i in range(1, modes // 128):
            tile = tile + part_sum[:, 128 * i : 128 * i + 128]
        cur[...] += tile
        own = off[modes:] + sw * small
        state[s] = own
        block = jnp.concatenate([off[0:modes], own], axis=0)
        bh, bl = split(block)
        qh[s] = bh[0:modes]
        ql[s] = bl[0:modes]
        factor_in(s).wait()
        h, l = split(fac[s])
        fh[s] = h
        fl[s] = l
        both = dot(jnp.concatenate([bh, bl], axis=0), h)
        off[...] = both[:total] + both[total:] + dot(bh, l)
        return carry

    lax.fori_loop(0, slabs, chain, 0)
    h, l = split(off[0:modes])
    th[...] = h
    tl[...] = l

    pl.semaphore_wait(barrier, n + groups - 2)

    def copy_to(source, target, send, receive, device):
        return pltpu.make_async_remote_copy(
            src_ref=source, dst_ref=target, send_sem=send, recv_sem=receive,
            device_id=(mine, device), device_id_type=MESH,
        )

    pair = copy_to(ps, pr, pair_s, pair_r, other)
    entry = copy_to(isend, irecv, is_, ir, other)
    leaving = copy_to(xsend, xrecv, xs, xr, other)
    joining = copy_to(jsend, jrecv, js, jr, other)

    def offset_to(j):
        return copy_to(osend, orecv.at[chip], os.at[j], our.at[chip], 2 * j + 1)

    def transfer_to(j, k):
        return copy_to(tsend, trecv.at[chip], ts.at[j], tr.at[chip], 2 * j + k)

    def exit_to(j):
        return copy_to(ysend, yrecv.at[chip], ys.at[j], yr.at[chip], 2 * j)

    def wait_transfer(j):
        copy_to(tsend, trecv.at[j], ts.at[j], tr.at[j], other).wait_recv()

    def wait_offset(j):
        copy_to(osend, orecv.at[j], os.at[j], our.at[j], other).wait_recv()

    def wait_exit(j):
        copy_to(ysend, yrecv.at[j], ys.at[j], yr.at[j], other).wait_recv()

    def put(ref, value, tile):
        ref[0:cols] = value
        ref[cols : cols + 8, 0:128] = tile
        ref[cols : cols + 8, 128:] = jnp.zeros((8, modes - 128), F32)

    inner = jnp.logical_and(chip > 0, chip < chips - 1)

    ps[0:total] = off[...]
    ps[total:, 0:128] = cur[...]
    ps[total:, 128:] = jnp.zeros((8, modes - 128), F32)
    pair.start()
    pair.wait_recv()
    cur[...] += pr[total:, 0:128]
    ctot[...] = cur[...]

    @pl.when(core == 1)
    def _():
        whole = mm(pr[0:total], th[...], tl[...])
        tsend[...] = whole[0:modes]
        put(osend, whole[modes:] + off[modes:], cur[...])
        for j in range(chips):
            @pl.when(j > chip)
            def _():
                offset_to(j).start()

        @pl.when(inner)
        def _():
            for j in range(chips):
                @pl.when(j > chip)
                def _():
                    transfer_to(j, 1).start()

                @pl.when(j < chip)
                def _():
                    transfer_to(j, 0).start()

    off[0:modes] = eye

    def suffix(i, carry):
        s = slabs - 1 - i
        u = mm(off[0:modes], fh[s], fl[s], True)
        off[0:modes] = u
        h, l = split(u)
        uh[s] = h
        ul[s] = l
        return carry

    lax.fori_loop(0, slabs, suffix, 0)

    inc[...] = jnp.zeros_like(inc)

    @pl.when(core == 1)
    def _():
        for j in range(chips - 1):
            @pl.when(chip > j)
            def _():
                if j > 0:
                    wait_transfer(j)
                wait_offset(j)
                if j == 0:
                    inc[...] = orecv[j, 0:cols]
                else:
                    h, l = split(trecv[j])
                    inc[...] = mm(inc[...], h, l) + orecv[j, 0:cols]
                ctot[...] += orecv[j, cols : cols + 8, 0:128]

        put(isend, inc[...], ctot[...])
        entry.start()
        h, l = split(pr[0:modes])
        inc[...] = mm(inc[...], h, l) + pr[modes:total]

    @pl.when(core == 0)
    def _():
        entry.wait_recv()
        inc[...] = irecv[0:cols]
        ctot[...] = irecv[cols : cols + 8, 0:128]

    pivots_in.wait()

    def weigh(s, leaves):
        now = state[s] + mm(inc[...], qh[s], ql[s])
        h, l = split(piv[s])
        weighted = mm(now, h, l)
        wt[s] = weighted
        return leaves + mm(weighted, qh[s], ql[s], True)

    exit_state = lax.fori_loop(0, slabs, weigh, jnp.zeros((cols, modes), F32), unroll=4)

    @pl.when(core == 1)
    def _():
        xsend[...] = exit_state
        leaving.start()

    @pl.when(core == 0)
    def _():
        leaving.wait_recv()

        @pl.when(chip > 0)
        def _():
            put(ysend, exit_state + mm(xrecv[...], th[...], tl[...], True), cur[...])
            for j in range(chips):
                @pl.when(j < chip)
                def _():
                    exit_to(j).start()

    def back(i, x):
        s = slabs - 1 - i
        x = wt[s] + mm(x, fh[s], fl[s], True)
        adj[s] = x
        return x

    lax.fori_loop(0, slabs, back, jnp.zeros((cols, modes), F32))

    def waves(b, carry):
        wg[b] = dot(wave[pl.ds(4 * b, 4)].reshape(4 * cols, modes), basis[...])
        return carry

    lax.fori_loop(0, slabs // 4, waves, 0)

    @pl.when(core == 0)
    def _():
        inc[...] = jnp.zeros_like(inc)
        for j in range(chips - 1, 0, -1):
            @pl.when(chip < j)
            def _():
                if j < chips - 1:
                    wait_transfer(j)
                wait_exit(j)
                if j == chips - 1:
                    inc[...] = yrecv[j, 0:cols]
                else:
                    h, l = split(trecv[j])
                    inc[...] = mm(inc[...], h, l, True) + yrecv[j, 0:cols]
                ctot[...] += yrecv[j, cols : cols + 8, 0:128]

        put(jsend, inc[...], ctot[...])
        joining.start()
        h, l = split(pr[0:modes])
        inc[...] = mm(inc[...], h, l, True) + xrecv[...]

    @pl.when(core == 1)
    def _():
        joining.wait_recv()
        inc[...] = jrecv[0:cols]
        ctot[...] = jrecv[cols : cols + 8, 0:128]

    def join(b, carry):
        for i in range(4):
            s = 4 * b + i
            h, l = split(adj[s] + mm(inc[...], uh[s], ul[s]))
            ahl[b, cols * i : cols * (i + 1)] = h
            ahl[b, cols * (4 + i) : cols * (5 + i)] = l
        return carry

    lax.fori_loop(0, slabs // 4, join, 0)

    copies = []
    for k in list(range(1, groups)) + [0]:
        peer = lax.rem(mine + k, groups)
        columns = pl.ds(pl.multiple_of(peer * part, 128), part)
        points = basis[:, columns]
        for b in range(slabs // 4):
            ag = dot(ahl[b], points)
            both = wg[b, :, columns] * (ag[: 4 * cols] + ag[4 * cols :])
            for i in range(4):
                esend[k, 4 * b + i : 4 * b + i + 1] = jnp.sum(
                    both[cols * i : cols * (i + 1)], axis=0, keepdims=True
                )
        esend[k, slabs : slabs + 8, 0:128] = ctot[...]
        if part > 128:
            esend[k, slabs : slabs + 8, 128:] = jnp.zeros((8, part - 128), F32)
        if k > 0:
            copies.append(
                pltpu.make_async_remote_copy(
                    src_ref=esend.at[k], dst_ref=erecv.at[k],
                    send_sem=es.at[k], recv_sem=er.at[k],
                    device_id=(peer, me), device_id_type=MESH,
                )
            )
            copies[-1].start()
    summed = esend[0]
    for k in range(1, groups):
        copies[k - 1].wait_recv()
        summed = summed + erecv[k]
    current = jnp.sum(summed[slabs : slabs + 8, 0:128])
    factor = (all_slabs * grid * (2.0 / small)) / current
    out[...] = summed[0:slabs] * factor
    for copy in copies:
        copy.wait_send()

    pair.wait_send()

    @pl.when(core == 1)
    def _():
        entry.wait_send()
        leaving.wait_send()
        for j in range(chips):
            @pl.when(j > chip)
            def _():
                offset_to(j).wait_send()

        @pl.when(inner)
        def _():
            for j in range(chips):
                @pl.when(j > chip)
                def _():
                    transfer_to(j, 1).wait_send()

                @pl.when(j < chip)
                def _():
                    transfer_to(j, 0).wait_send()

    @pl.when(core == 0)
    def _():
        joining.wait_send()
        for j in range(chips):
            @pl.when(j < chip)
            def _():
                exit_to(j).wait_send()


def local(wavefunction, injected_modes, factor_blocks, pivot_inverse, mode_velocity, energy_weight, mode_basis):
    n = lax.axis_size("slab")
    groups = lax.axis_size("energy")
    _, slabs, cols, modes = wavefunction.shape
    grid = mode_basis.shape[1]
    part = grid // groups
    vmem = pl.BlockSpec(memory_space=pltpu.VMEM)
    hbm = pl.BlockSpec(memory_space=pl.ANY)
    result = pl.pallas_call(
        functools.partial(kernel, n, groups),
        out_shape=jax.ShapeDtypeStruct((slabs, part), F32),
        in_specs=[vmem, vmem, hbm, hbm, vmem, vmem, vmem],
        out_specs=vmem,
        scratch_shapes=[
            pltpu.VMEM((slabs, modes, modes), F32),
            pltpu.VMEM((slabs, modes, modes), F32),
            pltpu.VMEM((slabs // 4, 8 * cols, modes), BF16),
            pltpu.SemaphoreType.DMA((slabs,)),
            pltpu.SemaphoreType.DMA,
            pltpu.VMEM((slabs, modes, modes), BF16),
            pltpu.VMEM((slabs, modes, modes), BF16),
            pltpu.VMEM((slabs, modes, modes), BF16),
            pltpu.VMEM((slabs, modes, modes), BF16),
            pltpu.VMEM((slabs, modes, modes), BF16),
            pltpu.VMEM((slabs, modes, modes), BF16),
            pltpu.VMEM((modes, modes), BF16),
            pltpu.VMEM((modes, modes), BF16),
            pltpu.VMEM((slabs, cols, modes), F32),
            pltpu.VMEM((slabs, cols, modes), F32),
            pltpu.VMEM((slabs, cols, modes), F32),
            pltpu.VMEM((slabs // 4, 4 * cols, grid), F32),
            pltpu.VMEM((modes + cols, modes), F32),
            pltpu.VMEM((cols, modes), F32),
            pltpu.VMEM((cols, modes), F32),
            pltpu.VMEM((8, 128), F32),
            pltpu.VMEM((8, 128), F32),
            pltpu.VMEM((modes + cols + 8, modes), F32),
            pltpu.VMEM((modes + cols + 8, modes), F32),
            pltpu.VMEM((cols + 8, modes), F32),
            pltpu.VMEM((n // 2, cols + 8, modes), F32),
            pltpu.VMEM((modes, modes), F32),
            pltpu.VMEM((n // 2, modes, modes), F32),
            pltpu.VMEM((cols + 8, modes), F32),
            pltpu.VMEM((cols + 8, modes), F32),
            pltpu.VMEM((cols, modes), F32),
            pltpu.VMEM((cols, modes), F32),
            pltpu.VMEM((cols + 8, modes), F32),
            pltpu.VMEM((n // 2, cols + 8, modes), F32),
            pltpu.VMEM((cols + 8, modes), F32),
            pltpu.VMEM((cols + 8, modes), F32),
            pltpu.VMEM((groups, slabs + 8, part), F32),
            pltpu.VMEM((groups, slabs + 8, part), F32),
            pltpu.SemaphoreType.DMA,
            pltpu.SemaphoreType.DMA,
            pltpu.SemaphoreType.DMA((n // 2,)),
            pltpu.SemaphoreType.DMA((n // 2,)),
            pltpu.SemaphoreType.DMA((n // 2,)),
            pltpu.SemaphoreType.DMA((n // 2,)),
            pltpu.SemaphoreType.DMA,
            pltpu.SemaphoreType.DMA,
            pltpu.SemaphoreType.DMA,
            pltpu.SemaphoreType.DMA,
            pltpu.SemaphoreType.DMA((n // 2,)),
            pltpu.SemaphoreType.DMA((n // 2,)),
            pltpu.SemaphoreType.DMA,
            pltpu.SemaphoreType.DMA,
            pltpu.SemaphoreType.DMA((groups,)),
            pltpu.SemaphoreType.DMA((groups,)),
        ],
        compiler_params=pltpu.CompilerParams(
            collective_id=0, has_side_effects=True, vmem_limit_bytes=60 * 1024 * 1024
        ),
    )(
        wavefunction[0],
        injected_modes,
        factor_blocks[0],
        pivot_inverse[0],
        mode_velocity,
        energy_weight.reshape(1, 1),
        mode_basis,
    )
    return result.T


def solution(mesh):
    return jax.shard_map(
        local,
        mesh=mesh,
        in_specs=(
            P("energy", "slab", None, None),
            P("energy", None),
            P("energy", "slab", None, None),
            P("energy", "slab", None, None),
            P("energy", None),
            P("energy"),
            P(),
        ),
        out_specs=P("energy", "slab"),
        check_vma=False,
    )
```

```python
import functools
import jax
import jax.numpy as jnp
from jax import lax
from jax.experimental import pallas as pl
from jax.experimental.pallas import tpu as pltpu
from jax.sharding import PartitionSpec as P

F32 = jnp.float32
BF16 = jnp.bfloat16
MESH = pl.DeviceIdType.MESH


def split(x):
    hi = x.astype(BF16)
    return hi, (x - hi.astype(F32)).astype(BF16)


def dot(a, b, transposed=False):
    return lax.dot_general(
        a, b, (((1,), (1 if transposed else 0,)), ((), ())), preferred_element_type=F32
    )


def mm(a, bh, bl, transposed=False):
    ah, al = split(a)
    rows = a.shape[0]
    both = dot(jnp.concatenate([ah, al], axis=0), bh, transposed)
    return both[:rows] + both[rows:] + dot(ah, bl, transposed)


def kernel(
    n, groups,
    wave, inj, fac_hbm, piv_hbm, vel, ew, basis,
    out,
    fac, piv, ahl, fac_sem, piv_sem,
    fh, fl, qh, ql, uh, ul, th, tl, state, wt, adj, wg, off, scaled_ref,
    inc, cur, ctot, ps, pr, osend, orecv, tsend, trecv, isend, irecv, xsend, xrecv,
    ysend, yrecv, jsend, jrecv, esend, erecv,
    pair_s, pair_r, os, our, ts, tr, is_, ir, xs, xr, ys, yr, js, jr, es, er,
):
    me = lax.axis_index("slab")
    mine = lax.axis_index("energy")
    slabs, cols, modes = wave.shape
    grid = basis.shape[1]
    part = grid // groups
    chips = n // 2
    chip = me // 2
    core = lax.rem(me, 2)
    other = me + 1 - 2 * core
    total = modes + cols
    all_slabs = n * slabs
    small = 2.0 / (all_slabs * cols * modes * groups * 4096.0)

    def factor_in(s):
        return pltpu.make_async_copy(fac_hbm.at[s], fac.at[s], fac_sem.at[s])

    for s in range(slabs):
        factor_in(s).start()
    pivots_in = pltpu.make_async_copy(piv_hbm, piv, piv_sem)
    pivots_in.start()

    barrier = pltpu.get_barrier_semaphore()

    for k in range(1, n):
        pl.semaphore_signal(
            barrier, inc=1, device_id=(mine, lax.rem(me + k, n)), device_id_type=MESH
        )
    for k in range(1, groups):
        peer = lax.rem(mine + k, groups)
        pl.semaphore_signal(barrier, inc=1, device_id=(peer, me), device_id_type=MESH)

    rows_at = lax.broadcasted_iota(jnp.int32, (cols, cols), 0)
    cols_at = lax.broadcasted_iota(jnp.int32, (cols, cols), 1)
    picked = jnp.sum(
        jnp.where(rows_at == cols_at, jnp.broadcast_to(inj[...].astype(F32), (cols, cols)), 0.0),
        axis=1, keepdims=True,
    )
    mode_at = lax.broadcasted_iota(jnp.int32, (cols, modes), 1).astype(F32)
    velocity = jnp.broadcast_to(vel[...], (cols, modes))
    at_injected = jnp.sum(jnp.where(mode_at == picked, velocity, 0.0), axis=1, keepdims=True)
    scaled_ref[...] = ew[...] * (1.0 / at_injected) * velocity

    eye = (
        lax.broadcasted_iota(jnp.int32, (modes, modes), 0)
        == lax.broadcasted_iota(jnp.int32, (modes, modes), 1)
    ).astype(F32)

    off[0:modes] = eye
    off[modes:] = jnp.zeros((cols, modes), F32)
    cur[...] = jnp.zeros_like(cur)

    def chain(s, carry):
        w = wave[s].astype(F32)
        sw = scaled_ref[...] * w
        sq = sw * w
        part_sum = sq[0:8]
        for i in range(1, cols // 8):
            part_sum = part_sum + sq[8 * i : 8 * i + 8]
        tile = part_sum[:, 0:128]
        for i in range(1, modes // 128):
            tile = tile + part_sum[:, 128 * i : 128 * i + 128]
        cur[...] += tile
        own = off[modes:] + sw * small
        state[s] = own
        block = jnp.concatenate([off[0:modes], own], axis=0)
        bh, bl = split(block)
        qh[s] = bh[0:modes]
        ql[s] = bl[0:modes]
        factor_in(s).wait()
        h, l = split(fac[s])
        fh[s] = h
        fl[s] = l
        both = dot(jnp.concatenate([bh, bl], axis=0), h)
        off[...] = both[:total] + both[total:] + dot(bh, l)
        return carry

    lax.fori_loop(0, slabs, chain, 0, unroll=4)
    h, l = split(off[0:modes])
    th[...] = h
    tl[...] = l

    pl.semaphore_wait(barrier, n + groups - 2)

    def copy_to(source, target, send, receive, device):
        return pltpu.make_async_remote_copy(
            src_ref=source, dst_ref=target, send_sem=send, recv_sem=receive,
            device_id=(mine, device), device_id_type=MESH,
        )

    pair = copy_to(ps, pr, pair_s, pair_r, other)
    entry = copy_to(isend, irecv, is_, ir, other)
    leaving = copy_to(xsend, xrecv, xs, xr, other)
    joining = copy_to(jsend, jrecv, js, jr, other)

    def offset_to(j):
        return copy_to(osend, orecv.at[chip], os.at[j], our.at[chip], 2 * j + 1)

    def transfer_to(j, k):
        return copy_to(tsend, trecv.at[chip], ts.at[j], tr.at[chip], 2 * j + k)

    def exit_to(j):
        return copy_to(ysend, yrecv.at[chip], ys.at[j], yr.at[chip], 2 * j)

    def wait_transfer(j):
        copy_to(tsend, trecv.at[j], ts.at[j], tr.at[j], other).wait_recv()

    def wait_offset(j):
        copy_to(osend, orecv.at[j], os.at[j], our.at[j], other).wait_recv()

    def wait_exit(j):
        copy_to(ysend, yrecv.at[j], ys.at[j], yr.at[j], other).wait_recv()

    def put(ref, value, tile):
        ref[0:cols] = value
        ref[cols : cols + 8, 0:128] = tile
        ref[cols : cols + 8, 128:] = jnp.zeros((8, modes - 128), F32)

    inner = jnp.logical_and(chip > 0, chip < chips - 1)

    ps[0:total] = off[...]
    ps[total:, 0:128] = cur[...]
    ps[total:, 128:] = jnp.zeros((8, modes - 128), F32)
    pair.start()
    pair.wait_recv()
    cur[...] += pr[total:, 0:128]
    ctot[...] = cur[...]

    @pl.when(core == 1)
    def _():
        whole = mm(pr[0:total], th[...], tl[...])
        tsend[...] = whole[0:modes]
        put(osend, whole[modes:] + off[modes:], cur[...])
        for j in range(chips):
            @pl.when(j > chip)
            def _():
                offset_to(j).start()

        @pl.when(inner)
        def _():
            for j in range(chips):
                @pl.when(j > chip)
                def _():
                    transfer_to(j, 1).start()

    off[0:modes] = eye

    def suffix(i, carry):
        s = slabs - 1 - i
        u = mm(off[0:modes], fh[s], fl[s], True)
        off[0:modes] = u
        h, l = split(u)
        uh[s] = h
        ul[s] = l
        return carry

    lax.fori_loop(0, slabs, suffix, 0, unroll=4)

    @pl.when(jnp.logical_and(core == 1, inner))
    def _():
        for j in range(chips):
            @pl.when(j < chip)
            def _():
                transfer_to(j, 0).start()

    inc[...] = jnp.zeros_like(inc)

    @pl.when(core == 1)
    def _():
        for j in range(chips - 1):
            @pl.when(chip > j)
            def _():
                if j > 0:
                    wait_transfer(j)
                wait_offset(j)
                if j == 0:
                    inc[...] = orecv[j, 0:cols]
                else:
                    h, l = split(trecv[j])
                    inc[...] = mm(inc[...], h, l) + orecv[j, 0:cols]
                ctot[...] += orecv[j, cols : cols + 8, 0:128]

        put(isend, inc[...], ctot[...])
        entry.start()
        h, l = split(pr[0:modes])
        inc[...] = mm(inc[...], h, l) + pr[modes:total]

    @pl.when(core == 0)
    def _():
        entry.wait_recv()
        inc[...] = irecv[0:cols]
        ctot[...] = irecv[cols : cols + 8, 0:128]

    pivots_in.wait()

    def weigh(s, leaves):
        now = state[s] + mm(inc[...], qh[s], ql[s])
        h, l = split(piv[s])
        weighted = mm(now, h, l)
        wt[s] = weighted
        return leaves + mm(weighted, qh[s], ql[s], True)

    exit_state = lax.fori_loop(0, slabs, weigh, jnp.zeros((cols, modes), F32), unroll=4)

    @pl.when(core == 1)
    def _():
        xsend[...] = exit_state
        leaving.start()

    @pl.when(core == 0)
    def _():
        leaving.wait_recv()

        @pl.when(chip > 0)
        def _():
            put(ysend, exit_state + mm(xrecv[...], th[...], tl[...], True), cur[...])
            for j in range(chips):
                @pl.when(j < chip)
                def _():
                    exit_to(j).start()

    def back(i, x):
        s = slabs - 1 - i
        x = wt[s] + mm(x, fh[s], fl[s], True)
        adj[s] = x
        return x

    lax.fori_loop(0, slabs, back, jnp.zeros((cols, modes), F32), unroll=4)

    def waves(b, carry):
        wg[b] = dot(wave[pl.ds(4 * b, 4)].reshape(4 * cols, modes), basis[...])
        return carry

    lax.fori_loop(0, slabs // 4, waves, 0)

    @pl.when(core == 0)
    def _():
        inc[...] = jnp.zeros_like(inc)
        for j in range(chips - 1, 0, -1):
            @pl.when(chip < j)
            def _():
                if j < chips - 1:
                    wait_transfer(j)
                wait_exit(j)
                if j == chips - 1:
                    inc[...] = yrecv[j, 0:cols]
                else:
                    h, l = split(trecv[j])
                    inc[...] = mm(inc[...], h, l, True) + yrecv[j, 0:cols]
                ctot[...] += yrecv[j, cols : cols + 8, 0:128]

        put(jsend, inc[...], ctot[...])
        joining.start()
        h, l = split(pr[0:modes])
        inc[...] = mm(inc[...], h, l, True) + xrecv[...]

    @pl.when(core == 1)
    def _():
        joining.wait_recv()
        inc[...] = jrecv[0:cols]
        ctot[...] = jrecv[cols : cols + 8, 0:128]

    def join(b, carry):
        for i in range(4):
            s = 4 * b + i
            h, l = split(adj[s] + mm(inc[...], uh[s], ul[s]))
            ahl[b, cols * i : cols * (i + 1)] = h
            ahl[b, cols * (4 + i) : cols * (5 + i)] = l
        return carry

    lax.fori_loop(0, slabs // 4, join, 0, unroll=2)

    copies = []
    for k in list(range(1, groups)) + [0]:
        peer = lax.rem(mine + k, groups)
        columns = pl.ds(pl.multiple_of(peer * part, 128), part)
        points = basis[:, columns]
        for b in range(slabs // 4):
            ag = dot(ahl[b], points)
            both = wg[b, :, columns] * (ag[: 4 * cols] + ag[4 * cols :])
            for i in range(4):
                esend[k, 4 * b + i : 4 * b + i + 1] = jnp.sum(
                    both[cols * i : cols * (i + 1)], axis=0, keepdims=True
                )
        esend[k, slabs : slabs + 8, 0:128] = ctot[...]
        if part > 128:
            esend[k, slabs : slabs + 8, 128:] = jnp.zeros((8, part - 128), F32)
        if k > 0:
            copies.append(
                pltpu.make_async_remote_copy(
                    src_ref=esend.at[k], dst_ref=erecv.at[k],
                    send_sem=es.at[k], recv_sem=er.at[k],
                    device_id=(peer, me), device_id_type=MESH,
                )
            )
            copies[-1].start()
    summed = esend[0]
    for k in range(1, groups):
        copies[k - 1].wait_recv()
        summed = summed + erecv[k]
    current = jnp.sum(summed[slabs : slabs + 8, 0:128])
    factor = (all_slabs * grid * (2.0 / small)) / current
    out[...] = summed[0:slabs] * factor
    for copy in copies:
        copy.wait_send()

    pair.wait_send()

    @pl.when(core == 1)
    def _():
        entry.wait_send()
        leaving.wait_send()
        for j in range(chips):
            @pl.when(j > chip)
            def _():
                offset_to(j).wait_send()

        @pl.when(inner)
        def _():
            for j in range(chips):
                @pl.when(j > chip)
                def _():
                    transfer_to(j, 1).wait_send()

                @pl.when(j < chip)
                def _():
                    transfer_to(j, 0).wait_send()

    @pl.when(core == 0)
    def _():
        joining.wait_send()
        for j in range(chips):
            @pl.when(j < chip)
            def _():
                exit_to(j).wait_send()


def local(wavefunction, injected_modes, factor_blocks, pivot_inverse, mode_velocity, energy_weight, mode_basis):
    n = lax.axis_size("slab")
    groups = lax.axis_size("energy")
    _, slabs, cols, modes = wavefunction.shape
    grid = mode_basis.shape[1]
    part = grid // groups
    vmem = pl.BlockSpec(memory_space=pltpu.VMEM)
    hbm = pl.BlockSpec(memory_space=pl.ANY)
    result = pl.pallas_call(
        functools.partial(kernel, n, groups),
        out_shape=jax.ShapeDtypeStruct((slabs, part), F32),
        in_specs=[vmem, vmem, hbm, hbm, vmem, vmem, vmem],
        out_specs=vmem,
        scratch_shapes=[
            pltpu.VMEM((slabs, modes, modes), F32),
            pltpu.VMEM((slabs, modes, modes), F32),
            pltpu.VMEM((slabs // 4, 8 * cols, modes), BF16),
            pltpu.SemaphoreType.DMA((slabs,)),
            pltpu.SemaphoreType.DMA,
            pltpu.VMEM((slabs, modes, modes), BF16),
            pltpu.VMEM((slabs, modes, modes), BF16),
            pltpu.VMEM((slabs, modes, modes), BF16),
            pltpu.VMEM((slabs, modes, modes), BF16),
            pltpu.VMEM((slabs, modes, modes), BF16),
            pltpu.VMEM((slabs, modes, modes), BF16),
            pltpu.VMEM((modes, modes), BF16),
            pltpu.VMEM((modes, modes), BF16),
            pltpu.VMEM((slabs, cols, modes), F32),
            pltpu.VMEM((slabs, cols, modes), F32),
            pltpu.VMEM((slabs, cols, modes), F32),
            pltpu.VMEM((slabs // 4, 4 * cols, grid), F32),
            pltpu.VMEM((modes + cols, modes), F32),
            pltpu.VMEM((cols, modes), F32),
            pltpu.VMEM((cols, modes), F32),
            pltpu.VMEM((8, 128), F32),
            pltpu.VMEM((8, 128), F32),
            pltpu.VMEM((modes + cols + 8, modes), F32),
            pltpu.VMEM((modes + cols + 8, modes), F32),
            pltpu.VMEM((cols + 8, modes), F32),
            pltpu.VMEM((n // 2, cols + 8, modes), F32),
            pltpu.VMEM((modes, modes), F32),
            pltpu.VMEM((n // 2, modes, modes), F32),
            pltpu.VMEM((cols + 8, modes), F32),
            pltpu.VMEM((cols + 8, modes), F32),
            pltpu.VMEM((cols, modes), F32),
            pltpu.VMEM((cols, modes), F32),
            pltpu.VMEM((cols + 8, modes), F32),
            pltpu.VMEM((n // 2, cols + 8, modes), F32),
            pltpu.VMEM((cols + 8, modes), F32),
            pltpu.VMEM((cols + 8, modes), F32),
            pltpu.VMEM((groups, slabs + 8, part), F32),
            pltpu.VMEM((groups, slabs + 8, part), F32),
            pltpu.SemaphoreType.DMA,
            pltpu.SemaphoreType.DMA,
            pltpu.SemaphoreType.DMA((n // 2,)),
            pltpu.SemaphoreType.DMA((n // 2,)),
            pltpu.SemaphoreType.DMA((n // 2,)),
            pltpu.SemaphoreType.DMA((n // 2,)),
            pltpu.SemaphoreType.DMA,
            pltpu.SemaphoreType.DMA,
            pltpu.SemaphoreType.DMA,
            pltpu.SemaphoreType.DMA,
            pltpu.SemaphoreType.DMA((n // 2,)),
            pltpu.SemaphoreType.DMA((n // 2,)),
            pltpu.SemaphoreType.DMA,
            pltpu.SemaphoreType.DMA,
            pltpu.SemaphoreType.DMA((groups,)),
            pltpu.SemaphoreType.DMA((groups,)),
        ],
        compiler_params=pltpu.CompilerParams(
            collective_id=0, has_side_effects=True, vmem_limit_bytes=60 * 1024 * 1024
        ),
    )(
        wavefunction[0],
        injected_modes,
        factor_blocks[0],
        pivot_inverse[0],
        mode_velocity,
        energy_weight.reshape(1, 1),
        mode_basis,
    )
    return result.T


def solution(mesh):
    return jax.shard_map(
        local,
        mesh=mesh,
        in_specs=(
            P("energy", "slab", None, None),
            P("energy", None),
            P("energy", "slab", None, None),
            P("energy", "slab", None, None),
            P("energy", None),
            P("energy"),
            P(),
        ),
        out_specs=P("energy", "slab"),
        check_vma=False,
    )
```

```python
import functools
import jax
import jax.numpy as jnp
from jax import lax
from jax.experimental import pallas as pl
from jax.experimental.pallas import tpu as pltpu
from jax.sharding import PartitionSpec as P

F32 = jnp.float32
BF16 = jnp.bfloat16
MESH = pl.DeviceIdType.MESH


def split(x):
    hi = x.astype(BF16)
    return hi, (x - hi.astype(F32)).astype(BF16)


def dot(a, b, transposed=False):
    return lax.dot_general(
        a, b, (((1,), (1 if transposed else 0,)), ((), ())), preferred_element_type=F32
    )


def mm(a, bh, bl, transposed=False):
    ah, al = split(a)
    rows = a.shape[0]
    both = dot(jnp.concatenate([ah, al], axis=0), bh, transposed)
    return both[:rows] + both[rows:] + dot(ah, bl, transposed)


def kernel(
    n, groups,
    wave, inj, fac_hbm, piv_hbm, vel, ew, basis,
    out,
    fac, piv, ahl, fac_sem, piv_sem, tah, tal, whole_off, incb,
    fh, fl, qh, ql, uh, ul, th, tl, state, wt, adj, wg, off, scaled_ref,
    inc, cur, ctot, ps, pr, osend, orecv, tsend, trecv, isend, irecv, xsend, xrecv,
    ysend, yrecv, jsend, jrecv, esend, erecv,
    pair_s, pair_r, os, our, ts, tr, is_, ir, xs, xr, ys, yr, js, jr, es, er,
):
    me = lax.axis_index("slab")
    mine = lax.axis_index("energy")
    slabs, cols, modes = wave.shape
    grid = basis.shape[1]
    part = grid // groups
    chips = n // 2
    chip = me // 2
    core = lax.rem(me, 2)
    other = me + 1 - 2 * core
    total = modes + cols
    half = slabs // 2
    all_slabs = n * slabs
    small = 2.0 / (all_slabs * cols * modes * groups * 4096.0)

    def factor_in(s):
        return pltpu.make_async_copy(fac_hbm.at[s], fac.at[s], fac_sem.at[s])

    for s in range(half):
        factor_in(s).start()
        factor_in(half + s).start()
    pivots_in = pltpu.make_async_copy(piv_hbm, piv, piv_sem)
    pivots_in.start()

    barrier = pltpu.get_barrier_semaphore()

    for k in range(1, n):
        pl.semaphore_signal(
            barrier, inc=1, device_id=(mine, lax.rem(me + k, n)), device_id_type=MESH
        )
    for k in range(1, groups):
        peer = lax.rem(mine + k, groups)
        pl.semaphore_signal(barrier, inc=1, device_id=(peer, me), device_id_type=MESH)

    rows_at = lax.broadcasted_iota(jnp.int32, (cols, cols), 0)
    cols_at = lax.broadcasted_iota(jnp.int32, (cols, cols), 1)
    picked = jnp.sum(
        jnp.where(rows_at == cols_at, jnp.broadcast_to(inj[...].astype(F32), (cols, cols)), 0.0),
        axis=1, keepdims=True,
    )
    mode_at = lax.broadcasted_iota(jnp.int32, (cols, modes), 1).astype(F32)
    velocity = jnp.broadcast_to(vel[...], (cols, modes))
    at_injected = jnp.sum(jnp.where(mode_at == picked, velocity, 0.0), axis=1, keepdims=True)
    scaled_ref[...] = ew[...] * (1.0 / at_injected) * velocity

    eye = (
        lax.broadcasted_iota(jnp.int32, (modes, modes), 0)
        == lax.broadcasted_iota(jnp.int32, (modes, modes), 1)
    ).astype(F32)

    for k in range(2):
        off[k, 0:modes] = eye
        off[k, modes:] = jnp.zeros((cols, modes), F32)
    cur[...] = jnp.zeros_like(cur)

    def chain(t, carry):
        blocks = []
        for k in range(2):
            s = k * half + t
            w = wave[s].astype(F32)
            sw = scaled_ref[...] * w
            sq = sw * w
            part_sum = sq[0:8]
            for i in range(1, cols // 8):
                part_sum = part_sum + sq[8 * i : 8 * i + 8]
            tile = part_sum[:, 0:128]
            for i in range(1, modes // 128):
                tile = tile + part_sum[:, 128 * i : 128 * i + 128]
            cur[...] += tile
            own = off[k, modes:] + sw * small
            state[s] = own
            bh, bl = split(jnp.concatenate([off[k, 0:modes], own], axis=0))
            qh[s] = bh[0:modes]
            ql[s] = bl[0:modes]
            factor_in(s).wait()
            h, l = split(fac[s])
            fh[s] = h
            fl[s] = l
            blocks.append((bh, bl, h, l))
        results = []
        for bh, bl, h, l in blocks:
            both = dot(jnp.concatenate([bh, bl], axis=0), h)
            results.append(both[:total] + both[total:] + dot(bh, l))
        for k in range(2):
            off[k] = results[k]
        return carry

    lax.fori_loop(0, half, chain, 0, unroll=2)
    h, l = split(off[0, 0:modes])
    tah[...] = h
    tal[...] = l
    h, l = split(off[1, 0:modes])
    joined = mm(off[0], h, l)
    h, l = split(joined[0:modes])
    th[...] = h
    tl[...] = l
    whole_off[...] = joined[modes:] + off[1, modes:]
    ps[0:modes] = joined[0:modes]
    ps[modes:total] = whole_off[...]

    pl.semaphore_wait(barrier, n + groups - 2)

    def copy_to(source, target, send, receive, device):
        return pltpu.make_async_remote_copy(
            src_ref=source, dst_ref=target, send_sem=send, recv_sem=receive,
            device_id=(mine, device), device_id_type=MESH,
        )

    pair = copy_to(ps, pr, pair_s, pair_r, other)
    entry = copy_to(isend, irecv, is_, ir, other)
    leaving = copy_to(xsend, xrecv, xs, xr, other)
    joining = copy_to(jsend, jrecv, js, jr, other)

    def offset_to(j):
        return copy_to(osend, orecv.at[chip], os.at[j], our.at[chip], 2 * j + 1)

    def transfer_to(j, k):
        return copy_to(tsend, trecv.at[chip], ts.at[j], tr.at[chip], 2 * j + k)

    def exit_to(j):
        return copy_to(ysend, yrecv.at[chip], ys.at[j], yr.at[chip], 2 * j)

    def wait_transfer(j):
        copy_to(tsend, trecv.at[j], ts.at[j], tr.at[j], other).wait_recv()

    def wait_offset(j):
        copy_to(osend, orecv.at[j], os.at[j], our.at[j], other).wait_recv()

    def wait_exit(j):
        copy_to(ysend, yrecv.at[j], ys.at[j], yr.at[j], other).wait_recv()

    def put(ref, value, tile):
        ref[0:cols] = value
        ref[cols : cols + 8, 0:128] = tile
        ref[cols : cols + 8, 128:] = jnp.zeros((8, modes - 128), F32)

    inner = jnp.logical_and(chip > 0, chip < chips - 1)

    ps[total:, 0:128] = cur[...]
    ps[total:, 128:] = jnp.zeros((8, modes - 128), F32)
    pair.start()
    pair.wait_recv()
    cur[...] += pr[total:, 0:128]
    ctot[...] = cur[...]

    @pl.when(core == 1)
    def _():
        whole = mm(pr[0:total], th[...], tl[...])
        tsend[...] = whole[0:modes]
        put(osend, whole[modes:] + whole_off[...], cur[...])
        for j in range(chips):
            @pl.when(j > chip)
            def _():
                offset_to(j).start()

        @pl.when(inner)
        def _():
            for j in range(chips):
                @pl.when(j > chip)
                def _():
                    transfer_to(j, 1).start()

    for k in range(2):
        off[k, 0:modes] = eye

    def suffix(i, carry):
        results = []
        for k in range(2):
            s = k * half + half - 1 - i
            results.append(mm(off[k, 0:modes], fh[s], fl[s], True))
        for k in range(2):
            s = k * half + half - 1 - i
            off[k, 0:modes] = results[k]
            h, l = split(results[k])
            uh[s] = h
            ul[s] = l
        return carry

    lax.fori_loop(0, half, suffix, 0, unroll=2)

    @pl.when(jnp.logical_and(core == 1, inner))
    def _():
        for j in range(chips):
            @pl.when(j < chip)
            def _():
                transfer_to(j, 0).start()

    inc[...] = jnp.zeros_like(inc)

    @pl.when(core == 1)
    def _():
        for j in range(chips - 1):
            @pl.when(chip > j)
            def _():
                if j > 0:
                    wait_transfer(j)
                wait_offset(j)
                if j == 0:
                    inc[...] = orecv[j, 0:cols]
                else:
                    h, l = split(trecv[j])
                    inc[...] = mm(inc[...], h, l) + orecv[j, 0:cols]
                ctot[...] += orecv[j, cols : cols + 8, 0:128]

        put(isend, inc[...], ctot[...])
        entry.start()
        h, l = split(pr[0:modes])
        inc[...] = mm(inc[...], h, l) + pr[modes:total]

    @pl.when(core == 0)
    def _():
        entry.wait_recv()
        inc[...] = irecv[0:cols]
        ctot[...] = irecv[cols : cols + 8, 0:128]

    pivots_in.wait()

    incb[...] = mm(inc[...], tah[...], tal[...]) + off[0, modes:]

    def weigh(t, leaves):
        left = []
        for k, entering in enumerate((inc, incb)):
            s = k * half + t
            now = state[s] + mm(entering[...], qh[s], ql[s])
            h, l = split(piv[s])
            weighted = mm(now, h, l)
            wt[s] = weighted
            left.append(leaves[k] + mm(weighted, qh[s], ql[s], True))
        return tuple(left)

    nothing = jnp.zeros((cols, modes), F32)
    leaves = lax.fori_loop(0, half, weigh, (nothing, nothing), unroll=2)
    exit_state = leaves[0] + mm(leaves[1], tah[...], tal[...], True)

    @pl.when(core == 1)
    def _():
        xsend[...] = exit_state
        leaving.start()

    @pl.when(core == 0)
    def _():
        leaving.wait_recv()

        @pl.when(chip > 0)
        def _():
            put(ysend, exit_state + mm(xrecv[...], th[...], tl[...], True), cur[...])
            for j in range(chips):
                @pl.when(j < chip)
                def _():
                    exit_to(j).start()

    def back(i, held):
        left = []
        for k in range(2):
            s = k * half + half - 1 - i
            x = wt[s] + mm(held[k], fh[s], fl[s], True)
            adj[s] = x
            left.append(x)
        return tuple(left)

    lax.fori_loop(0, half, back, (nothing, nothing), unroll=2)

    def waves(b, carry):
        wg[b] = dot(wave[pl.ds(4 * b, 4)].reshape(4 * cols, modes), basis[...])
        return carry

    lax.fori_loop(0, slabs // 4, waves, 0)

    @pl.when(core == 0)
    def _():
        inc[...] = jnp.zeros_like(inc)
        for j in range(chips - 1, 0, -1):
            @pl.when(chip < j)
            def _():
                if j < chips - 1:
                    wait_transfer(j)
                wait_exit(j)
                if j == chips - 1:
                    inc[...] = yrecv[j, 0:cols]
                else:
                    h, l = split(trecv[j])
                    inc[...] = mm(inc[...], h, l, True) + yrecv[j, 0:cols]
                ctot[...] += yrecv[j, cols : cols + 8, 0:128]

        put(jsend, inc[...], ctot[...])
        joining.start()
        h, l = split(pr[0:modes])
        inc[...] = mm(inc[...], h, l, True) + xrecv[...]

    @pl.when(core == 1)
    def _():
        joining.wait_recv()
        inc[...] = jrecv[0:cols]
        ctot[...] = jrecv[cols : cols + 8, 0:128]

    incb[...] = adj[half] + mm(inc[...], uh[half], ul[half])

    for b in range(slabs // 4):
        for i in range(4):
            s = 4 * b + i
            entering = incb if s < half else inc
            h, l = split(adj[s] + mm(entering[...], uh[s], ul[s]))
            ahl[b, cols * i : cols * (i + 1)] = h
            ahl[b, cols * (4 + i) : cols * (5 + i)] = l

    copies = []
    for k in list(range(1, groups)) + [0]:
        peer = lax.rem(mine + k, groups)
        columns = pl.ds(pl.multiple_of(peer * part, 128), part)
        points = basis[:, columns]
        for b in range(slabs // 4):
            ag = dot(ahl[b], points)
            both = wg[b, :, columns] * (ag[: 4 * cols] + ag[4 * cols :])
            for i in range(4):
                esend[k, 4 * b + i : 4 * b + i + 1] = jnp.sum(
                    both[cols * i : cols * (i + 1)], axis=0, keepdims=True
                )
        esend[k, slabs : slabs + 8, 0:128] = ctot[...]
        if part > 128:
            esend[k, slabs : slabs + 8, 128:] = jnp.zeros((8, part - 128), F32)
        if k > 0:
            copies.append(
                pltpu.make_async_remote_copy(
                    src_ref=esend.at[k], dst_ref=erecv.at[k],
                    send_sem=es.at[k], recv_sem=er.at[k],
                    device_id=(peer, me), device_id_type=MESH,
                )
            )
            copies[-1].start()
    summed = esend[0]
    for k in range(1, groups):
        copies[k - 1].wait_recv()
        summed = summed + erecv[k]
    current = jnp.sum(summed[slabs : slabs + 8, 0:128])
    factor = (all_slabs * grid * (2.0 / small)) / current
    out[...] = summed[0:slabs] * factor
    for copy in copies:
        copy.wait_send()

    pair.wait_send()

    @pl.when(core == 1)
    def _():
        entry.wait_send()
        leaving.wait_send()
        for j in range(chips):
            @pl.when(j > chip)
            def _():
                offset_to(j).wait_send()

        @pl.when(inner)
        def _():
            for j in range(chips):
                @pl.when(j > chip)
                def _():
                    transfer_to(j, 1).wait_send()

                @pl.when(j < chip)
                def _():
                    transfer_to(j, 0).wait_send()

    @pl.when(core == 0)
    def _():
        joining.wait_send()
        for j in range(chips):
            @pl.when(j < chip)
            def _():
                exit_to(j).wait_send()


def local(wavefunction, injected_modes, factor_blocks, pivot_inverse, mode_velocity, energy_weight, mode_basis):
    n = lax.axis_size("slab")
    groups = lax.axis_size("energy")
    _, slabs, cols, modes = wavefunction.shape
    grid = mode_basis.shape[1]
    part = grid // groups
    vmem = pl.BlockSpec(memory_space=pltpu.VMEM)
    hbm = pl.BlockSpec(memory_space=pl.ANY)
    result = pl.pallas_call(
        functools.partial(kernel, n, groups),
        out_shape=jax.ShapeDtypeStruct((slabs, part), F32),
        in_specs=[vmem, vmem, hbm, hbm, vmem, vmem, vmem],
        out_specs=vmem,
        scratch_shapes=[
            pltpu.VMEM((slabs, modes, modes), F32),
            pltpu.VMEM((slabs, modes, modes), F32),
            pltpu.VMEM((slabs // 4, 8 * cols, modes), BF16),
            pltpu.SemaphoreType.DMA((slabs,)),
            pltpu.SemaphoreType.DMA,
            pltpu.VMEM((modes, modes), BF16),
            pltpu.VMEM((modes, modes), BF16),
            pltpu.VMEM((cols, modes), F32),
            pltpu.VMEM((cols, modes), F32),
            pltpu.VMEM((slabs, modes, modes), BF16),
            pltpu.VMEM((slabs, modes, modes), BF16),
            pltpu.VMEM((slabs, modes, modes), BF16),
            pltpu.VMEM((slabs, modes, modes), BF16),
            pltpu.VMEM((slabs, modes, modes), BF16),
            pltpu.VMEM((slabs, modes, modes), BF16),
            pltpu.VMEM((modes, modes), BF16),
            pltpu.VMEM((modes, modes), BF16),
            pltpu.VMEM((slabs, cols, modes), F32),
            pltpu.VMEM((slabs, cols, modes), F32),
            pltpu.VMEM((slabs, cols, modes), F32),
            pltpu.VMEM((slabs // 4, 4 * cols, grid), F32),
            pltpu.VMEM((2, modes + cols, modes), F32),
            pltpu.VMEM((cols, modes), F32),
            pltpu.VMEM((cols, modes), F32),
            pltpu.VMEM((8, 128), F32),
            pltpu.VMEM((8, 128), F32),
            pltpu.VMEM((modes + cols + 8, modes), F32),
            pltpu.VMEM((modes + cols + 8, modes), F32),
            pltpu.VMEM((cols + 8, modes), F32),
            pltpu.VMEM((n // 2, cols + 8, modes), F32),
            pltpu.VMEM((modes, modes), F32),
            pltpu.VMEM((n // 2, modes, modes), F32),
            pltpu.VMEM((cols + 8, modes), F32),
            pltpu.VMEM((cols + 8, modes), F32),
            pltpu.VMEM((cols, modes), F32),
            pltpu.VMEM((cols, modes), F32),
            pltpu.VMEM((cols + 8, modes), F32),
            pltpu.VMEM((n // 2, cols + 8, modes), F32),
            pltpu.VMEM((cols + 8, modes), F32),
            pltpu.VMEM((cols + 8, modes), F32),
            pltpu.VMEM((groups, slabs + 8, part), F32),
            pltpu.VMEM((groups, slabs + 8, part), F32),
            pltpu.SemaphoreType.DMA,
            pltpu.SemaphoreType.DMA,
            pltpu.SemaphoreType.DMA((n // 2,)),
            pltpu.SemaphoreType.DMA((n // 2,)),
            pltpu.SemaphoreType.DMA((n // 2,)),
            pltpu.SemaphoreType.DMA((n // 2,)),
            pltpu.SemaphoreType.DMA,
            pltpu.SemaphoreType.DMA,
            pltpu.SemaphoreType.DMA,
            pltpu.SemaphoreType.DMA,
            pltpu.SemaphoreType.DMA((n // 2,)),
            pltpu.SemaphoreType.DMA((n // 2,)),
            pltpu.SemaphoreType.DMA,
            pltpu.SemaphoreType.DMA,
            pltpu.SemaphoreType.DMA((groups,)),
            pltpu.SemaphoreType.DMA((groups,)),
        ],
        compiler_params=pltpu.CompilerParams(
            collective_id=0, has_side_effects=True, vmem_limit_bytes=60 * 1024 * 1024
        ),
    )(
        wavefunction[0],
        injected_modes,
        factor_blocks[0],
        pivot_inverse[0],
        mode_velocity,
        energy_weight.reshape(1, 1),
        mode_basis,
    )
    return result.T


def solution(mesh):
    return jax.shard_map(
        local,
        mesh=mesh,
        in_specs=(
            P("energy", "slab", None, None),
            P("energy", None),
            P("energy", "slab", None, None),
            P("energy", "slab", None, None),
            P("energy", None),
            P("energy"),
            P(),
        ),
        out_specs=P("energy", "slab"),
        check_vma=False,
    )
```

```python
import functools
import jax
import jax.numpy as jnp
from jax import lax
from jax.experimental import pallas as pl
from jax.experimental.pallas import tpu as pltpu
from jax.sharding import PartitionSpec as P

F32 = jnp.float32
BF16 = jnp.bfloat16
MESH = pl.DeviceIdType.MESH


def split(x):
    hi = x.astype(BF16)
    return hi, (x - hi.astype(F32)).astype(BF16)


def dot(a, b, transposed=False):
    return lax.dot_general(
        a, b, (((1,), (1 if transposed else 0,)), ((), ())), preferred_element_type=F32
    )


def mm(a, bh, bl, transposed=False):
    ah, al = split(a)
    rows = a.shape[0]
    both = dot(jnp.concatenate([ah, al], axis=0), bh, transposed)
    return both[:rows] + both[rows:] + dot(ah, bl, transposed)


def kernel(
    n, groups,
    wave, inj, fac_hbm, piv_hbm, vel, ew, basis,
    out,
    fac, piv, ahl, fac_sem, piv_sem, tah, tal, whole_off, incb,
    fh, fl, qh, ql, uh, ul, th, tl, state, wt, adj, wg, off, scaled_ref,
    inc, cur, ctot, ps, pr, osend, orecv, tsend, trecv, isend, irecv, xsend, xrecv,
    ysend, yrecv, jsend, jrecv, esend, erecv,
    pair_s, pair_r, os, our, ts, tr, is_, ir, xs, xr, ys, yr, js, jr, es, er,
):
    me = lax.axis_index("slab")
    mine = lax.axis_index("energy")
    slabs, cols, modes = wave.shape
    grid = basis.shape[1]
    part = grid // groups
    chips = n // 2
    chip = me // 2
    core = lax.rem(me, 2)
    other = me + 1 - 2 * core
    total = modes + cols
    half = slabs // 2
    all_slabs = n * slabs
    small = 2.0 / (all_slabs * cols * modes * groups * 4096.0)

    def factor_in(s):
        return pltpu.make_async_copy(fac_hbm.at[s], fac.at[s], fac_sem.at[s])

    for s in range(half):
        factor_in(s).start()
        factor_in(half + s).start()
    pivots_in = pltpu.make_async_copy(piv_hbm, piv, piv_sem)
    pivots_in.start()

    barrier = pltpu.get_barrier_semaphore()

    for k in range(1, n):
        pl.semaphore_signal(
            barrier, inc=1, device_id=(mine, lax.rem(me + k, n)), device_id_type=MESH
        )
    for k in range(1, groups):
        peer = lax.rem(mine + k, groups)
        pl.semaphore_signal(barrier, inc=1, device_id=(peer, me), device_id_type=MESH)

    rows_at = lax.broadcasted_iota(jnp.int32, (cols, cols), 0)
    cols_at = lax.broadcasted_iota(jnp.int32, (cols, cols), 1)
    picked = jnp.sum(
        jnp.where(rows_at == cols_at, jnp.broadcast_to(inj[...].astype(F32), (cols, cols)), 0.0),
        axis=1, keepdims=True,
    )
    mode_at = lax.broadcasted_iota(jnp.int32, (cols, modes), 1).astype(F32)
    velocity = jnp.broadcast_to(vel[...], (cols, modes))
    at_injected = jnp.sum(jnp.where(mode_at == picked, velocity, 0.0), axis=1, keepdims=True)
    scaled_ref[...] = ew[...] * (1.0 / at_injected) * velocity

    eye = (
        lax.broadcasted_iota(jnp.int32, (modes, modes), 0)
        == lax.broadcasted_iota(jnp.int32, (modes, modes), 1)
    ).astype(F32)

    for k in range(2):
        off[k, 0:modes] = eye
        off[k, modes:] = jnp.zeros((cols, modes), F32)
    cur[...] = jnp.zeros_like(cur)

    def chain(t, carry):
        blocks = []
        for k in range(2):
            s = k * half + t
            w = wave[s].astype(F32)
            sw = scaled_ref[...] * w
            sq = sw * w
            part_sum = sq[0:8]
            for i in range(1, cols // 8):
                part_sum = part_sum + sq[8 * i : 8 * i + 8]
            tile = part_sum[:, 0:128]
            for i in range(1, modes // 128):
                tile = tile + part_sum[:, 128 * i : 128 * i + 128]
            cur[...] += tile
            own = off[k, modes:] + sw * small
            state[s] = own
            bh, bl = split(jnp.concatenate([off[k, 0:modes], own], axis=0))
            qh[s] = bh[0:modes]
            ql[s] = bl[0:modes]
            factor_in(s).wait()
            h, l = split(fac[s])
            fh[s] = h
            fl[s] = l
            blocks.append((bh, bl, h, l))
        results = []
        for bh, bl, h, l in blocks:
            both = dot(jnp.concatenate([bh, bl], axis=0), h)
            results.append(both[:total] + both[total:] + dot(bh, l))
        for k in range(2):
            off[k] = results[k]
        return carry

    lax.fori_loop(0, half, chain, 0, unroll=2)
    h, l = split(off[0, 0:modes])
    tah[...] = h
    tal[...] = l
    h, l = split(off[1, 0:modes])
    joined = mm(off[0], h, l)
    h, l = split(joined[0:modes])
    th[...] = h
    tl[...] = l
    whole_off[...] = joined[modes:] + off[1, modes:]
    ps[0:modes] = joined[0:modes]
    ps[modes:total] = whole_off[...]

    pl.semaphore_wait(barrier, n + groups - 2)

    def copy_to(source, target, send, receive, device):
        return pltpu.make_async_remote_copy(
            src_ref=source, dst_ref=target, send_sem=send, recv_sem=receive,
            device_id=(mine, device), device_id_type=MESH,
        )

    pair = copy_to(ps, pr, pair_s, pair_r, other)
    entry = copy_to(isend, irecv, is_, ir, other)
    leaving = copy_to(xsend, xrecv, xs, xr, other)
    joining = copy_to(jsend, jrecv, js, jr, other)

    def offset_to(j):
        return copy_to(osend, orecv.at[chip], os.at[j], our.at[chip], 2 * j + 1)

    def transfer_to(j, k):
        return copy_to(tsend, trecv.at[chip], ts.at[j], tr.at[chip], 2 * j + k)

    def exit_to(j):
        return copy_to(ysend, yrecv.at[chip], ys.at[j], yr.at[chip], 2 * j)

    def wait_transfer(j):
        copy_to(tsend, trecv.at[j], ts.at[j], tr.at[j], other).wait_recv()

    def wait_offset(j):
        copy_to(osend, orecv.at[j], os.at[j], our.at[j], other).wait_recv()

    def wait_exit(j):
        copy_to(ysend, yrecv.at[j], ys.at[j], yr.at[j], other).wait_recv()

    def put(ref, value, tile):
        ref[0:cols] = value
        ref[cols : cols + 8, 0:128] = tile
        ref[cols : cols + 8, 128:] = jnp.zeros((8, modes - 128), F32)

    inner = jnp.logical_and(chip > 0, chip < chips - 1)

    ps[total:, 0:128] = cur[...]
    ps[total:, 128:] = jnp.zeros((8, modes - 128), F32)
    pair.start()
    pair.wait_recv()
    cur[...] += pr[total:, 0:128]
    ctot[...] = cur[...]

    @pl.when(core == 1)
    def _():
        whole = mm(pr[0:total], th[...], tl[...])
        tsend[...] = whole[0:modes]
        put(osend, whole[modes:] + whole_off[...], cur[...])
        for j in range(chips):
            @pl.when(j > chip)
            def _():
                offset_to(j).start()

        @pl.when(inner)
        def _():
            for j in range(chips):
                @pl.when(j > chip)
                def _():
                    transfer_to(j, 1).start()

    for k in range(2):
        off[k, 0:modes] = eye

    def suffix(i, carry):
        results = []
        for k in range(2):
            s = k * half + half - 1 - i
            results.append(mm(off[k, 0:modes], fh[s], fl[s], True))
        for k in range(2):
            s = k * half + half - 1 - i
            off[k, 0:modes] = results[k]
            h, l = split(results[k])
            uh[s] = h
            ul[s] = l
        return carry

    lax.fori_loop(0, half, suffix, 0, unroll=2)

    @pl.when(jnp.logical_and(core == 1, inner))
    def _():
        for j in range(chips):
            @pl.when(j < chip)
            def _():
                transfer_to(j, 0).start()

    def waves(b, carry):
        wg[b] = dot(wave[pl.ds(4 * b, 4)].reshape(4 * cols, modes), basis[...])
        return carry

    lax.fori_loop(0, slabs // 4, waves, 0)

    inc[...] = jnp.zeros_like(inc)

    @pl.when(core == 1)
    def _():
        for j in range(chips - 1):
            @pl.when(chip > j)
            def _():
                if j > 0:
                    wait_transfer(j)
                wait_offset(j)
                if j == 0:
                    inc[...] = orecv[j, 0:cols]
                else:
                    h, l = split(trecv[j])
                    inc[...] = mm(inc[...], h, l) + orecv[j, 0:cols]
                ctot[...] += orecv[j, cols : cols + 8, 0:128]

        put(isend, inc[...], ctot[...])
        entry.start()
        h, l = split(pr[0:modes])
        inc[...] = mm(inc[...], h, l) + pr[modes:total]

    @pl.when(core == 0)
    def _():
        entry.wait_recv()
        inc[...] = irecv[0:cols]
        ctot[...] = irecv[cols : cols + 8, 0:128]

    pivots_in.wait()

    incb[...] = mm(inc[...], tah[...], tal[...]) + off[0, modes:]

    def weigh(t, leaves):
        left = []
        for k, entering in enumerate((inc, incb)):
            s = k * half + t
            now = state[s] + mm(entering[...], qh[s], ql[s])
            h, l = split(piv[s])
            weighted = mm(now, h, l)
            wt[s] = weighted
            left.append(leaves[k] + mm(weighted, qh[s], ql[s], True))
        return tuple(left)

    nothing = jnp.zeros((cols, modes), F32)
    leaves = lax.fori_loop(0, half, weigh, (nothing, nothing), unroll=2)
    exit_state = leaves[0] + mm(leaves[1], tah[...], tal[...], True)

    @pl.when(core == 1)
    def _():
        xsend[...] = exit_state
        leaving.start()

    @pl.when(core == 0)
    def _():
        leaving.wait_recv()

        @pl.when(chip > 0)
        def _():
            put(ysend, exit_state + mm(xrecv[...], th[...], tl[...], True), cur[...])
            for j in range(chips):
                @pl.when(j < chip)
                def _():
                    exit_to(j).start()

    def back(i, held):
        left = []
        for k in range(2):
            s = k * half + half - 1 - i
            x = wt[s] + mm(held[k], fh[s], fl[s], True)
            adj[s] = x
            left.append(x)
        return tuple(left)

    lax.fori_loop(0, half, back, (nothing, nothing), unroll=2)

    @pl.when(core == 0)
    def _():
        inc[...] = jnp.zeros_like(inc)
        for j in range(chips - 1, 0, -1):
            @pl.when(chip < j)
            def _():
                if j < chips - 1:
                    wait_transfer(j)
                wait_exit(j)
                if j == chips - 1:
                    inc[...] = yrecv[j, 0:cols]
                else:
                    h, l = split(trecv[j])
                    inc[...] = mm(inc[...], h, l, True) + yrecv[j, 0:cols]
                ctot[...] += yrecv[j, cols : cols + 8, 0:128]

        put(jsend, inc[...], ctot[...])
        joining.start()
        h, l = split(pr[0:modes])
        inc[...] = mm(inc[...], h, l, True) + xrecv[...]

    @pl.when(core == 1)
    def _():
        joining.wait_recv()
        inc[...] = jrecv[0:cols]
        ctot[...] = jrecv[cols : cols + 8, 0:128]

    incb[...] = adj[half] + mm(inc[...], uh[half], ul[half])

    for b in range(slabs // 4):
        for i in range(4):
            s = 4 * b + i
            entering = incb if s < half else inc
            h, l = split(adj[s] + mm(entering[...], uh[s], ul[s]))
            ahl[b, cols * i : cols * (i + 1)] = h
            ahl[b, cols * (4 + i) : cols * (5 + i)] = l

    copies = []
    for k in list(range(1, groups)) + [0]:
        peer = lax.rem(mine + k, groups)
        columns = pl.ds(pl.multiple_of(peer * part, 128), part)
        points = basis[:, columns]
        for b in range(slabs // 4):
            ag = dot(ahl[b], points)
            both = wg[b, :, columns] * (ag[: 4 * cols] + ag[4 * cols :])
            for i in range(4):
                esend[k, 4 * b + i : 4 * b + i + 1] = jnp.sum(
                    both[cols * i : cols * (i + 1)], axis=0, keepdims=True
                )
        esend[k, slabs : slabs + 8, 0:128] = ctot[...]
        if part > 128:
            esend[k, slabs : slabs + 8, 128:] = jnp.zeros((8, part - 128), F32)
        if k > 0:
            copies.append(
                pltpu.make_async_remote_copy(
                    src_ref=esend.at[k], dst_ref=erecv.at[k],
                    send_sem=es.at[k], recv_sem=er.at[k],
                    device_id=(peer, me), device_id_type=MESH,
                )
            )
            copies[-1].start()
    summed = esend[0]
    for k in range(1, groups):
        copies[k - 1].wait_recv()
        summed = summed + erecv[k]
    current = jnp.sum(summed[slabs : slabs + 8, 0:128])
    factor = (all_slabs * grid * (2.0 / small)) / current
    out[...] = summed[0:slabs] * factor
    for copy in copies:
        copy.wait_send()

    pair.wait_send()

    @pl.when(core == 1)
    def _():
        entry.wait_send()
        leaving.wait_send()
        for j in range(chips):
            @pl.when(j > chip)
            def _():
                offset_to(j).wait_send()

        @pl.when(inner)
        def _():
            for j in range(chips):
                @pl.when(j > chip)
                def _():
                    transfer_to(j, 1).wait_send()

                @pl.when(j < chip)
                def _():
                    transfer_to(j, 0).wait_send()

    @pl.when(core == 0)
    def _():
        joining.wait_send()
        for j in range(chips):
            @pl.when(j < chip)
            def _():
                exit_to(j).wait_send()


def local(wavefunction, injected_modes, factor_blocks, pivot_inverse, mode_velocity, energy_weight, mode_basis):
    n = lax.axis_size("slab")
    groups = lax.axis_size("energy")
    _, slabs, cols, modes = wavefunction.shape
    grid = mode_basis.shape[1]
    part = grid // groups
    vmem = pl.BlockSpec(memory_space=pltpu.VMEM)
    hbm = pl.BlockSpec(memory_space=pl.ANY)
    result = pl.pallas_call(
        functools.partial(kernel, n, groups),
        out_shape=jax.ShapeDtypeStruct((slabs, part), F32),
        in_specs=[vmem, vmem, hbm, hbm, vmem, vmem, vmem],
        out_specs=vmem,
        scratch_shapes=[
            pltpu.VMEM((slabs, modes, modes), F32),
            pltpu.VMEM((slabs, modes, modes), F32),
            pltpu.VMEM((slabs // 4, 8 * cols, modes), BF16),
            pltpu.SemaphoreType.DMA((slabs,)),
            pltpu.SemaphoreType.DMA,
            pltpu.VMEM((modes, modes), BF16),
            pltpu.VMEM((modes, modes), BF16),
            pltpu.VMEM((cols, modes), F32),
            pltpu.VMEM((cols, modes), F32),
            pltpu.VMEM((slabs, modes, modes), BF16),
            pltpu.VMEM((slabs, modes, modes), BF16),
            pltpu.VMEM((slabs, modes, modes), BF16),
            pltpu.VMEM((slabs, modes, modes), BF16),
            pltpu.VMEM((slabs, modes, modes), BF16),
            pltpu.VMEM((slabs, modes, modes), BF16),
            pltpu.VMEM((modes, modes), BF16),
            pltpu.VMEM((modes, modes), BF16),
            pltpu.VMEM((slabs, cols, modes), F32),
            pltpu.VMEM((slabs, cols, modes), F32),
            pltpu.VMEM((slabs, cols, modes), F32),
            pltpu.VMEM((slabs // 4, 4 * cols, grid), F32),
            pltpu.VMEM((2, modes + cols, modes), F32),
            pltpu.VMEM((cols, modes), F32),
            pltpu.VMEM((cols, modes), F32),
            pltpu.VMEM((8, 128), F32),
            pltpu.VMEM((8, 128), F32),
            pltpu.VMEM((modes + cols + 8, modes), F32),
            pltpu.VMEM((modes + cols + 8, modes), F32),
            pltpu.VMEM((cols + 8, modes), F32),
            pltpu.VMEM((n // 2, cols + 8, modes), F32),
            pltpu.VMEM((modes, modes), F32),
            pltpu.VMEM((n // 2, modes, modes), F32),
            pltpu.VMEM((cols + 8, modes), F32),
            pltpu.VMEM((cols + 8, modes), F32),
            pltpu.VMEM((cols, modes), F32),
            pltpu.VMEM((cols, modes), F32),
            pltpu.VMEM((cols + 8, modes), F32),
            pltpu.VMEM((n // 2, cols + 8, modes), F32),
            pltpu.VMEM((cols + 8, modes), F32),
            pltpu.VMEM((cols + 8, modes), F32),
            pltpu.VMEM((groups, slabs + 8, part), F32),
            pltpu.VMEM((groups, slabs + 8, part), F32),
            pltpu.SemaphoreType.DMA,
            pltpu.SemaphoreType.DMA,
            pltpu.SemaphoreType.DMA((n // 2,)),
            pltpu.SemaphoreType.DMA((n // 2,)),
            pltpu.SemaphoreType.DMA((n // 2,)),
            pltpu.SemaphoreType.DMA((n // 2,)),
            pltpu.SemaphoreType.DMA,
            pltpu.SemaphoreType.DMA,
            pltpu.SemaphoreType.DMA,
            pltpu.SemaphoreType.DMA,
            pltpu.SemaphoreType.DMA((n // 2,)),
            pltpu.SemaphoreType.DMA((n // 2,)),
            pltpu.SemaphoreType.DMA,
            pltpu.SemaphoreType.DMA,
            pltpu.SemaphoreType.DMA((groups,)),
            pltpu.SemaphoreType.DMA((groups,)),
        ],
        compiler_params=pltpu.CompilerParams(
            collective_id=0, has_side_effects=True, vmem_limit_bytes=60 * 1024 * 1024
        ),
    )(
        wavefunction[0],
        injected_modes,
        factor_blocks[0],
        pivot_inverse[0],
        mode_velocity,
        energy_weight.reshape(1, 1),
        mode_basis,
    )
    return result.T


def solution(mesh):
    return jax.shard_map(
        local,
        mesh=mesh,
        in_specs=(
            P("energy", "slab", None, None),
            P("energy", None),
            P("energy", "slab", None, None),
            P("energy", "slab", None, None),
            P("energy", None),
            P("energy"),
            P(),
        ),
        out_specs=P("energy", "slab"),
        check_vma=False,
    )
```
